512 devices in a mesh: modes: 16 (over y, x_lo, core), sites: 32 (over x_hi, z).
Axes of the slice: x: 4 (x_hi: 2, x_lo: 2; x = x_hi * 2 + x_lo), y: 4, z: 16, core: 2. Of those that a mesh axis runs over, the one named last changes fastest.
Arguments:
- wave_state: float32 [4, 128, 131072], P(None, 'modes', 'sites'), may hold values from -6 to 6
- potential: float32 [131072], P('sites'), may hold values from -0.5 to 0.5
- spin_angle: float32 [131072], P('sites'), may hold values from -3.140625 to 3.140625
- magnet: float32 [3, 131072], P(None, 'sites'), may hold values from -0.6 to 0.6
- magnetic_mask: int32 [131072], P('sites'), may hold values 0 or 1
- mode_weight: float32 [128], P('modes'), may hold values from 0.5 to 2
- source_amp: float32 [4, 128], P(None, 'modes'), may hold values from -6 to 6
- mode_group: int32 [128], P('modes'), may hold values from 0 to 7
- energies: float32 [8], replicated, may hold values from -2 to 2
- lead_site: int32 [128], P('modes'), may hold values from 0 to 131071
Outputs:
- next_state: float32 [4, 128, 131072], P(None, 'modes', 'sites')
- densities: float32 [5, 131072], P(None, 'sites')
- magnet_next: float32 [3, 131072], P(None, 'sites')
The draws below stay inside these ranges and needn't reach their ends.
All inputs are finite; a program needn't handle non-finite values. No bound on the sum of `magnetic_mask` on one device may be relied on, other than what follows from the above.
Results may differ from the reference program's by a relative error of at most 0.0001.
Values sent between devices are 32-bit elements; how exact they have to be, the bound alone decides.
A program may use at most 64 MiB of HBM per device.

```python
import math
import jax
import jax.numpy as jnp
from jax import lax

MODE_DEV = 8
GROUPS = 8
MODES = 128
NSITES = 131072


def place_ends(entries, stream_key, smallest, top_value):
    longest = entries.shape.index(max(entries.shape))
    spots = []
    for shift in (0, 1):
        where = [jax.random.randint(jax.random.fold_in(stream_key, axis), (), 0, length) for axis, length in enumerate(entries.shape)]
        where[longest] = (where[longest] + shift) % entries.shape[longest]
        spots.append(tuple(where))
    return entries.at[spots[0]].set(smallest).at[spots[1]].set(top_value)


def block_scale(key, extent, pieces, least, largest):
    def one(position, blocks):
        steps = jax.random.uniform(jax.random.fold_in(jax.random.fold_in(key, 6), position), (blocks,), jnp.float32, least / len(pieces), largest / len(pieces))
        return jnp.repeat(jnp.exp(steps), extent[position] // blocks).reshape((-1,) + (1,) * (len(extent) - position - 1))

    loudness = one(*pieces[0])
    for cut in pieces[1:]:
        loudness = loudness * one(*cut)
    return loudness


def centred(stream_key, dims, scale, limit, shards=(), kind=jnp.bfloat16):
    entries = jax.random.normal(stream_key, dims, jnp.float32) * scale
    if len(shards) > 0:
        entries = block_scale(stream_key, dims, shards, -0.22, 0.18) * entries
    return jnp.clip(entries, min=-limit, max=limit).astype(kind)


def setup_inputs(seed: int = 0) -> dict:
    seeds = jax.random.split(jax.random.key(seed), 11)
    return {
        "wave_state": centred(seeds[0], (4, MODES, NSITES), 1.0, 6.0, ((1, 16), (2, 32)), jnp.float32),
        "potential": jnp.clip(jax.random.uniform(seeds[1], (NSITES,), jnp.float32, -0.5, 0.5) * block_scale(seeds[1], (NSITES,), ((0, 32),), -0.4, 0.0), -0.5, 0.5),
        "spin_angle": jnp.clip(jax.random.uniform(seeds[2], (NSITES,), jnp.float32, -3.140625, 3.140625), -3.140625, 3.140625),
        "magnet": jnp.clip(jax.random.uniform(seeds[3], (3, NSITES), jnp.float32, -0.6, 0.6) * block_scale(seeds[3], (3, NSITES), ((1, 32),), -0.4, 0.0), -0.6, 0.6),
        "magnetic_mask": place_ends((jax.random.randint(seeds[4], (NSITES,), 0, 2) < 1).astype(jnp.int32), jax.random.fold_in(seeds[4], 1), 0, 1),
        "mode_weight": jnp.clip(jnp.exp(math.log(2.0) - 1.3862944 * jax.random.uniform(seeds[5], (MODES,), jnp.float32) ** block_scale(seeds[5], (MODES,), ((0, 16),), -0.2, 0.2)), 0.5, 2.0),
        "source_amp": centred(seeds[6], (4, MODES), 1.0, 6.0, ((1, 16),), jnp.float32),
        "mode_group": place_ends(jax.random.randint(seeds[7], (MODES,), 0, GROUPS), jax.random.fold_in(seeds[7], 1), 0, GROUPS - 1).astype(jnp.int32),
        "energies": jnp.clip(jax.random.uniform(seeds[8], (GROUPS,), jnp.float32, -2.0, 2.0), -2.0, 2.0),
        "lead_site": place_ends(jax.random.randint(seeds[9], (MODES,), 0, NSITES), jax.random.fold_in(seeds[9], 1), 0, NSITES - 1).astype(jnp.int32),
    }


time_step = 0.6
start_time = 10.0
exchange_coupling = 0.5

def rotate_back(spinor, cosine, sine_term):
    shaped = spinor.reshape((2, 2) + spinor.shape[1:])
    spin_up = shaped[:, 0]
    spin_down = shaped[:, 1]
    turned = jnp.stack([cosine * spin_up + sine_term * spin_down, cosine * spin_down - sine_term * spin_up], axis=1)
    return turned.reshape(spinor.shape)

def rotate_fore(spinor, cosine, sine_term):
    shaped = spinor.reshape((2, 2) + spinor.shape[1:])
    spin_up = shaped[:, 0]
    spin_down = shaped[:, 1]
    turned = jnp.stack([cosine * spin_up - sine_term * spin_down, sine_term * spin_up + cosine * spin_down], axis=1)
    return turned.reshape(spinor.shape)

def exchange_term(spinor, sd_field):
    up_real, down_real, up_imag, down_imag = (spinor[0], spinor[1], spinor[2], spinor[3])
    field_x, field_y, field_z = (sd_field[0], sd_field[1], sd_field[2])
    out_up_real = field_z * up_real + field_x * down_real + field_y * down_imag
    out_down_real = field_x * up_real - field_y * up_imag - field_z * down_real
    out_up_imag = field_z * up_imag + field_x * down_imag - field_y * down_real
    out_down_imag = field_x * up_imag + field_y * up_real - field_z * down_imag
    return jnp.stack([out_up_real, out_down_real, out_up_imag, out_down_imag])

def source_field(offset, amplitude, energy, region):
    phase_angle = energy * (start_time + offset)
    cosine_phase = jnp.cos(phase_angle)
    sine_phase = jnp.sin(phase_angle)
    amp_real = amplitude[0:2]
    amp_imag = amplitude[2:4]
    real_part = amp_real * cosine_phase + amp_imag * sine_phase
    imag_part = amp_imag * cosine_phase - amp_real * sine_phase
    joined = jnp.concatenate([real_part, imag_part], axis=0)
    return joined[:, :, None] * region[None]

def rate(spinor, left_w, right_w, cosine, sine_term, potential, sd_field, source):
    hamil_term = potential * spinor + exchange_term(spinor, sd_field) - rotate_fore(left_w + right_w, cosine, sine_term) + source
    return jnp.concatenate([hamil_term[2:], -hamil_term[:2]], axis=0)

def densities_of(spinor, right_w, cosine, sine_term, weight_vec):
    up_real, down_real, up_imag, down_imag = (spinor[0], spinor[1], spinor[2], spinor[3])
    hopped = rotate_fore(right_w, cosine, sine_term)
    charge = up_real * up_real + down_real * down_real + up_imag * up_imag + down_imag * down_imag
    spin_x = 2.0 * (up_real * down_real + up_imag * down_imag)
    spin_y = 2.0 * (up_real * down_imag - up_imag * down_real)
    spin_z = up_real * up_real + up_imag * up_imag - down_real * down_real - down_imag * down_imag
    current = 2.0 * (up_real * hopped[2] + down_real * hopped[3] - up_imag * hopped[0] - down_imag * hopped[1])
    stacked = jnp.stack([charge, spin_x, spin_y, spin_z, current])
    return lax.optimization_barrier(jnp.sum(stacked * weight_vec[None, :, None], axis=1))

def advance(magnet, mask_float, totals):
    field_h = exchange_coupling * totals[1:4]
    torque = jnp.stack([magnet[1] * field_h[2] - magnet[2] * field_h[1], magnet[2] * field_h[0] - magnet[0] * field_h[2], magnet[0] * field_h[1] - magnet[1] * field_h[0]])
    return magnet - time_step * (mask_float * torque)

def reference(wave_state, potential, spin_angle, magnet, magnetic_mask, mode_weight, source_amp, mode_group, energies, lead_site):
    sites_all = wave_state.shape[2]
    modes_all = wave_state.shape[1]
    region_span = sites_all // 8
    cosine = jnp.cos(spin_angle)
    sine_term = jnp.sin(spin_angle)
    mask_float = magnetic_mask.astype(jnp.float32)
    sd_field = exchange_coupling * mask_float * magnet
    energy_all = lax.optimization_barrier(jnp.sum(jnp.where(mode_group[:, None] == jnp.arange(GROUPS, dtype=jnp.int32)[None, :], energies[None, :], jnp.zeros_like(energies)[None, :]), axis=1))
    positions = jnp.arange(sites_all, dtype=jnp.int32)
    block_size = MODE_DEV
    block_count = modes_all // block_size

    def one_block(block_index, state_pair):
        next_all, density_sum = state_pair
        offset_mode = (block_index * block_size).astype(jnp.int32)
        spinor = lax.dynamic_slice_in_dim(wave_state, offset_mode, block_size, 1)
        amplitude = lax.dynamic_slice_in_dim(source_amp, offset_mode, block_size, 1)
        energy = lax.dynamic_slice_in_dim(energy_all, offset_mode, block_size, 0)
        lead_block = lax.dynamic_slice_in_dim(lead_site, offset_mode, block_size, 0)
        weight_block = lax.dynamic_slice_in_dim(mode_weight, offset_mode, block_size, 0)
        region = ((positions[None, :] >= lead_block[:, None]) & (positions[None, :] < lead_block[:, None] + region_span)).astype(jnp.float32)

        def slope(spin_state, offset):
            weighted = rotate_back(spin_state, cosine, sine_term)
            padded = jnp.pad(weighted, ((0, 0), (0, 0), (1, 1)))
            source = source_field(offset, amplitude, energy, region)
            return (rate(spin_state, padded[..., :-2], padded[..., 2:], cosine, sine_term, potential, sd_field, source), padded)
        slope_one, padded_one = slope(spinor, 0.0)
        slope_two, ignored = slope(spinor + 0.5 * time_step * slope_one, 0.5 * time_step)
        slope_three, ignored = slope(spinor + 0.5 * time_step * slope_two, 0.5 * time_step)
        slope_four, ignored = slope(spinor + time_step * slope_three, time_step)
        advanced = spinor + time_step / 6.0 * (slope_one + 2.0 * slope_two + 2.0 * slope_three + slope_four)
        density_sum = density_sum + densities_of(spinor, padded_one[..., 2:], cosine, sine_term, weight_block)
        next_all = lax.dynamic_update_slice_in_dim(next_all, advanced, offset_mode, 1)
        return (next_all, density_sum)
    next_state, density_sum = lax.fori_loop(0, block_count, one_block, (jnp.zeros_like(wave_state), jnp.zeros((5, sites_all), jnp.float32)))
    root_scale = 1.0 / math.sqrt(modes_all)
    row_scale = jnp.array([1.0 / modes_all, root_scale, root_scale, root_scale, root_scale], jnp.float32)
    totals = density_sum * row_scale[:, None]
    magnet_next = advance(magnet, mask_float, totals)
    return (next_state, totals, magnet_next)
```

```python
import functools
import math

import jax
import jax.numpy as jnp
from jax import lax
from jax.experimental import pallas as pl
from jax.experimental.pallas import tpu as pltpu
from jax.sharding import PartitionSpec as P

time_step = 0.6
start_time = 10.0
exchange_coupling = 0.5
MESH = pl.DeviceIdType.MESH
LANES = 128

E4 = time_step**4 / 24.0
STAGE_WEIGHT = [
    24.0 / time_step**4,
    24.0 / time_step**3,
    12.0 / time_step**2,
    4.0 / time_step,
]


def apply_stage(y, left, right, coef, base, weight, src, masks):
    ur, dr, ui, di = y
    a_up, a_dn, fx, fy = coef
    near = [l + r for l, r in zip(left, right)]
    h_ur = a_up * ur + fx * dr + fy * di - near[0]
    h_dr = a_dn * dr + fx * ur - fy * ui - near[1]
    h_ui = a_up * ui + fx * di - fy * dr - near[2]
    h_di = a_dn * di + fx * ui + fy * ur - near[3]
    cm, sm = masks
    src_ur = cm * src[0] + sm * src[1]
    src_dr = cm * src[1] - sm * src[0]
    src_ui = cm * src[2] + sm * src[3]
    src_di = cm * src[3] - sm * src[2]
    return [
        (weight * base[0] + src_ur) + h_ui,
        (weight * base[1] + src_dr) + h_di,
        (weight * base[2] + src_ui) - h_ur,
        (weight * base[3] + src_di) - h_dr,
    ]


def kernel(
    nm,
    ns,
    sites,
    wave_hbm,
    pot_hbm,
    ang_hbm,
    mag_hbm,
    mask_hbm,
    wt_hbm,
    amp_hbm,
    grp_hbm,
    en_hbm,
    lead_hbm,
    next_out,
    dens_out,
    magn_out,
    wave,
    pot,
    ang,
    mag,
    mask,
    wt,
    amp,
    grp,
    en,
    lead,
    cos_d,
    sin_d,
    cos2_d,
    sin2_d,
    half_d,
    par,
    w,
    ya,
    yb,
    coef,
    cmask,
    edge_l,
    edge_r,
    halo_l,
    halo_r,
    part,
    slots,
    own,
    sums,
    in_sem,
    halo_send,
    halo_recv,
    rs_send,
    rs_recv,
    ag_send,
    ag_recv,
):
    chunks = sites // LANES
    share = sites // nm
    unroll = 4
    me = lax.axis_index("modes")
    tile = lax.axis_index("sites")
    left_id = lax.rem(tile + ns - 1, ns)
    right_id = lax.rem(tile + 1, ns)
    peers = [lax.rem(me + k, nm) for k in range(1, nm)]

    barrier = pltpu.get_barrier_semaphore()
    for peer in peers:
        pl.semaphore_signal(barrier, inc=1, device_id={"modes": peer}, device_id_type=MESH)
    for side in (left_id, right_id):
        pl.semaphore_signal(barrier, inc=1, device_id={"sites": side}, device_id_type=MESH)

    fetches = [
        pltpu.make_async_copy(src, dst, in_sem.at[i])
        for i, (src, dst) in enumerate(
            [
                (wt_hbm, wt),
                (amp_hbm, amp),
                (grp_hbm, grp),
                (en_hbm, en),
                (lead_hbm, lead),
                (ang_hbm, ang),
                (pot_hbm, pot),
                (mag_hbm, mag),
                (mask_hbm, mask),
                (wave_hbm, wave),
            ]
        )
    ]
    for fetch in fetches:
        fetch.start()
    for fetch in fetches[:5]:
        fetch.wait()

    group = grp[...]
    energy_row = en[...]
    energy = jnp.zeros(group.shape, jnp.float32)
    for g in range(energy_row.shape[1]):
        energy = energy + jnp.where(group == g, energy_row[:, g : g + 1], 0.0)
    amp_re = amp[0:2, :]
    amp_im = amp[2:4, :]
    rate = []
    for offset in (0.0, 0.5 * time_step, time_step):
        phase = energy * (start_time + offset)
        cosine = jnp.cos(phase)
        sine = jnp.sin(phase)
        rate.append(
            (
                amp_im * cosine - amp_re * sine,
                -(amp_re * cosine + amp_im * sine),
            )
        )
    mixes = [
        [time_step / 6.0, 4.0 * time_step / 6.0, time_step / 6.0],
        [time_step / 6.0, 2.0 * time_step / 6.0, 0.0],
        [time_step / 6.0, time_step / 6.0, 0.0],
        [time_step / 4.0, 0.0, 0.0],
    ]
    modes = group.shape[1]
    diag = lax.broadcasted_iota(jnp.int32, (modes, modes), 0) == lax.broadcasted_iota(
        jnp.int32, (modes, modes), 1
    )

    def column(row):
        spread = jnp.where(diag, jnp.broadcast_to(row, (modes, modes)), 0.0)
        return jnp.broadcast_to(jnp.sum(spread, axis=1, keepdims=True), (modes, LANES))

    for k in range(4):
        for half in range(2):
            mixed = sum(
                (STAGE_WEIGHT[k] * mixes[k][t]) * rate[t][half]
                for t in range(3)
                if mixes[k][t] != 0.0
            )
            for spin in range(2):
                par[4 * k + 2 * half + spin] = column(mixed[spin : spin + 1, :])
    par[16] = column(wt[...])
    par[17] = column(lead[...].astype(jnp.float32))

    for fetch in fetches[5:9]:
        fetch.wait()
    angle = ang[...]
    cosine = jnp.cos(angle)
    sine = jnp.sin(angle)
    cos_d[...] = cosine
    sin_d[...] = sine
    cos2_d[...] = 1.0 - 2.0 * sine * sine
    sin2_d[...] = 2.0 * sine * cosine
    half_d[...] = exchange_coupling * mask[...].astype(jnp.float32)

    zero = jnp.zeros((8, LANES), jnp.float32)
    for buf in (w, ya, yb):
        for c in range(4):
            buf[c, :, 0:LANES] = zero
            buf[c, :, LANES + sites : 2 * LANES + sites] = zero
    lane = lax.broadcasted_iota(jnp.int32, (8, LANES), 1)
    first = lane == 0
    last = lane == LANES - 1
    span = float(sites * ns // 8)

    def in_region(position):
        away = position.astype(jnp.float32) - par[17]
        return (away >= 0.0) & (away < span)

    def row(ref, i):
        return jnp.broadcast_to(ref[pl.ds(i, 1), :], (8, LANES))

    fetches[9].wait()

    def at(c, shift=0):
        return pl.ds(pl.multiple_of(c * LANES, LANES) + shift * LANES, LANES)

    def rotate(block, carry):
        for u in range(unroll):
            c = block * unroll + u
            cs = row(cos_d, c)
            sn = row(sin_d, c)
            c2 = row(cos2_d, c)
            s2 = row(sin2_d, c)
            half = row(half_d, c)
            field = [half * jnp.broadcast_to(mag[i : i + 1, at(c)], (8, LANES)) for i in range(3)]
            v = row(pot, c)
            fz = c2 * field[2] + s2 * field[0]
            coef[0, :, at(c)] = v + fz
            coef[1, :, at(c)] = v - fz
            coef[2, :, at(c)] = c2 * field[0] - s2 * field[2]
            coef[3, :, at(c)] = field[1]
            coef[4, :, at(c)] = cs
            coef[5, :, at(c)] = sn
            inside = in_region(tile * sites + c * LANES + lane)
            cmask[0, :, at(c)] = jnp.where(inside, cs, 0.0)
            cmask[1, :, at(c)] = jnp.where(inside, sn, 0.0)
            for half_i in range(2):
                up = wave[2 * half_i, :, at(c)]
                down = wave[2 * half_i + 1, :, at(c)]
                w[2 * half_i, :, at(c, 1)] = cs * up + sn * down
                w[2 * half_i + 1, :, at(c, 1)] = cs * down - sn * up
        return carry

    lax.fori_loop(0, chunks // unroll, rotate, 0)

    sub = lax.broadcasted_iota(jnp.int32, (8, LANES), 0)
    for edge, c in ((edge_l, 0), (edge_r, chunks - 1)):
        for i in range(4):
            edge[i] = w[i, :, (c + 1) * LANES : (c + 2) * LANES]
        rows = zero
        for i in range(6):
            rows = jnp.where(sub == i, coef[i, :, c * LANES : (c + 1) * LANES], rows)
        edge[4] = rows

    pl.semaphore_wait(barrier, nm + 1)
    to_left = pltpu.make_async_remote_copy(
        src_ref=edge_l,
        dst_ref=halo_r,
        send_sem=halo_send.at[0],
        recv_sem=halo_recv.at[0],
        device_id={"sites": left_id},
        device_id_type=MESH,
    )
    to_right = pltpu.make_async_remote_copy(
        src_ref=edge_r,
        dst_ref=halo_l,
        send_sem=halo_send.at[1],
        recv_sem=halo_recv.at[1],
        device_id={"sites": right_id},
        device_id_type=MESH,
    )
    to_left.start()
    to_right.start()

    all_modes = float(modes * nm)
    root = 1.0 / math.sqrt(all_modes)
    weight = par[16]

    def current(wc, wn, weight):
        after = [jnp.where(first, n, c) for c, n in zip(wc, wn)]
        after = [pltpu.roll(a, LANES - 1, 1) for a in after]
        return weight * (
            wc[0] * after[2] - wc[2] * after[0] + (wc[1] * after[3] - wc[3] * after[1])
        )

    def down_sum(x):
        return jnp.sum(x, axis=0, keepdims=True)

    def density(block, carry):
        wc = [w[i, :, at(block * unroll, 1)] for i in range(4)]
        for u in range(unroll):
            c = block * unroll + u
            wn = [w[i, :, at(c, 2)] for i in range(4)]
            ur, dr, ui, di = [wave[i, :, at(c)] for i in range(4)]
            wur, wdr, wui, wdi = [weight * x for x in (ur, dr, ui, di)]
            up = down_sum(wur * ur + wui * ui)
            dn = down_sum(wdr * dr + wdi * di)
            sx = down_sum(wur * dr + wui * di)
            sy = down_sum(wur * di - wui * dr)
            cur = down_sum(current(wc, wn, weight))
            rows = [
                (up + dn) * (1.0 / all_modes),
                sx * (2.0 * root),
                sy * (2.0 * root),
                (up - dn) * root,
                cur * (2.0 * root),
            ]
            packed = zero
            for i, r in enumerate(rows):
                packed = jnp.where(sub == i, jnp.broadcast_to(r, (8, LANES)), packed)
            part[:, at(c)] = packed
            wc = wn
        return carry

    lax.fori_loop(0, chunks // unroll, density, 0)

    scatter = []
    for k, peer in enumerate(peers):
        scatter.append(
            pltpu.make_async_remote_copy(
                src_ref=part.at[:, pl.ds(pl.multiple_of(peer * share, LANES), share)],
                dst_ref=slots.at[k],
                send_sem=rs_send,
                recv_sem=rs_recv,
                device_id={"modes": peer},
                device_id_type=MESH,
            )
        )
        scatter[-1].start()

    def stage_pass(src_ref, dst_ref, k):
        def body(block, carry):
            def load(c, shift):
                return [src_ref[i, :, at(c, shift)] for i in range(4)]

            c0 = block * unroll
            prev = load(c0, 0)
            here = load(c0, 1)
            for u in range(unroll):
                c = c0 + u
                after = load(c, 2)
                lefts = [pltpu.roll(jnp.where(last, p, h), 1, 1) for p, h in zip(prev, here)]
                rights = [
                    pltpu.roll(jnp.where(first, a, h), LANES - 1, 1) for a, h in zip(after, here)
                ]
                base = here if k == 3 else [w[i, :, at(c, 1)] for i in range(4)]
                out = apply_stage(
                    here,
                    lefts,
                    rights,
                    [coef[i, :, at(c)] for i in range(4)],
                    base,
                    STAGE_WEIGHT[k],
                    [par[4 * k + i] for i in range(4)],
                    [cmask[0, :, at(c)], cmask[1, :, at(c)]],
                )
                if k > 0:
                    for i in range(4):
                        dst_ref[i, :, at(c, 1)] = out[i]
                else:
                    cs = E4 * coef[4, :, at(c)]
                    sn = E4 * coef[5, :, at(c)]
                    for h in range(2):
                        next_out[2 * h, :, at(c)] = cs * out[2 * h] - sn * out[2 * h + 1]
                        next_out[2 * h + 1, :, at(c)] = sn * out[2 * h] + cs * out[2 * h + 1]
                prev, here = here, after
            return carry

        lax.fori_loop(0, chunks // unroll, body, 0)

    stage_pass(w, ya, 3)
    stage_pass(ya, yb, 2)
    stage_pass(yb, ya, 1)
    stage_pass(ya, None, 0)

    to_left.wait_recv()
    to_right.wait_recv()
    has_left = tile > 0
    has_right = tile < ns - 1
    base = []
    coefs = []
    masks = []
    alive = []
    for where in range(4):
        if where in (0, 3):
            halo = halo_l if where == 0 else halo_r
            there = has_left if where == 0 else has_right
            keep = jnp.full((8, LANES), there.astype(jnp.int32)) > 0
            alive.append(keep)
            base.append([jnp.where(keep, halo[i], 0.0) for i in range(4)])
            rows = [jnp.broadcast_to(halo[4, i : i + 1, :], (8, LANES)) for i in range(6)]
            coefs.append(rows[:4])
            start = tile * sites + (-LANES if where == 0 else sites)
            inside = in_region(start + lane)
            masks.append([jnp.where(inside, rows[4], 0.0), jnp.where(inside, rows[5], 0.0)])
        else:
            c = 0 if where == 1 else chunks - 1
            cut = slice(c * LANES, (c + 1) * LANES)
            alive.append(None)
            base.append([w[i, :, (c + 1) * LANES : (c + 2) * LANES] for i in range(4)])
            coefs.append([coef[i, :, cut] for i in range(4)])
            masks.append([cmask[0, :, cut], cmask[1, :, cut]])

    extra = down_sum(current(base[2], base[3], weight)) * (2.0 * root)
    extra = jnp.where(last & (sub == 5), jnp.broadcast_to(extra, (8, LANES)), 0.0)

    scatter_all = pltpu.make_async_copy(slots, slots, rs_recv)
    scatter_all.wait()
    total = part[:, pl.ds(pl.multiple_of(me * share, LANES), share)]
    for k in range(nm - 1):
        total = total + slots[k]
    own[...] = total
    own[:, share - LANES : share] = total[:, share - LANES : share] + extra
    mine = pl.ds(pl.multiple_of(me * share, LANES), share)
    gather = []
    for k, peer in enumerate(peers):
        gather.append(
            pltpu.make_async_remote_copy(
                src_ref=own,
                dst_ref=sums.at[me],
                send_sem=ag_send,
                recv_sem=ag_recv,
                device_id={"modes": peer},
                device_id_type=MESH,
            )
        )
        gather[-1].start()
    sums[me] = own[...]

    y = base
    for k in (3, 2, 1, 0):
        out = []
        for where in range(4):
            prev, here, after = y[(where + 3) % 4], y[where], y[(where + 1) % 4]
            lefts = [pltpu.roll(jnp.where(last, p, h), 1, 1) for p, h in zip(prev, here)]
            rights = [
                pltpu.roll(jnp.where(first, a, h), LANES - 1, 1) for a, h in zip(after, here)
            ]
            new = apply_stage(
                here,
                lefts,
                rights,
                coefs[where],
                base[where],
                STAGE_WEIGHT[k],
                [par[4 * k + i] for i in range(4)],
                masks[where],
            )
            if alive[where] is not None:
                new = [jnp.where(alive[where], x, 0.0) for x in new]
            out.append(new)
        y = out
    for where, c in ((1, 0), (2, chunks - 1)):
        cut = slice(c * LANES, (c + 1) * LANES)
        cs = E4 * coef[4, :, cut]
        sn = E4 * coef[5, :, cut]
        fresh = lane < 4 if where == 1 else lane >= LANES - 4
        for h in range(2):
            up = cs * y[where][2 * h] - sn * y[where][2 * h + 1]
            down = sn * y[where][2 * h] + cs * y[where][2 * h + 1]
            next_out[2 * h, :, cut] = jnp.where(fresh, up, next_out[2 * h, :, cut])
            next_out[2 * h + 1, :, cut] = jnp.where(fresh, down, next_out[2 * h + 1, :, cut])

    pltpu.make_async_copy(slots, slots, ag_recv).wait()
    bond = sums[0, :, share - LANES : share]
    for q in range(1, nm):
        bond = bond + sums[q, :, share - LANES : share]
    bond = jnp.where(last[0:1] & has_right, bond[5:6, :], 0.0)
    for q in range(nm):
        cut = slice(q * share, (q + 1) * share)
        got = sums[q]
        if q == nm - 1:
            dens_out[0:4, cut] = got[0:4, :]
            dens_out[4:5, q * share : (q + 1) * share - LANES] = got[4:5, : share - LANES]
            dens_out[4:5, (q + 1) * share - LANES : (q + 1) * share] = (
                got[4:5, share - LANES :] + bond
            )
        else:
            dens_out[:, cut] = got[0:5, :]
        turn = (time_step * exchange_coupling) * jnp.concatenate(
            [
                mask[q * share // LANES + i : q * share // LANES + i + 1, :].astype(jnp.float32)
                for i in range(share // LANES)
            ],
            axis=1,
        )
        m = [mag[i : i + 1, cut] for i in range(3)]
        hx, hy, hz = got[1:2, :], got[2:3, :], got[3:4, :]
        magn_out[0:1, cut] = m[0] - turn * (m[1] * hz - m[2] * hy)
        magn_out[1:2, cut] = m[1] - turn * (m[2] * hx - m[0] * hz)
        magn_out[2:3, cut] = m[2] - turn * (m[0] * hy - m[1] * hx)

    to_left.wait_send()
    to_right.wait_send()
    pltpu.make_async_copy(slots, slots, rs_send).wait()
    pltpu.make_async_copy(slots, slots, ag_send).wait()


def hand_out(next_v, dens_v, magn_v, next_out, dens_out, magn_out, sem):
    copies = [
        pltpu.make_async_copy(src, dst, sem.at[i])
        for i, (src, dst) in enumerate(
            [(next_v, next_out), (dens_v, dens_out), (magn_v, magn_out)]
        )
    ]
    for copy in copies:
        copy.start()
    for copy in copies:
        copy.wait()


def solution(mesh):
    nm = mesh.shape["modes"]
    ns = mesh.shape["sites"]

    def local(
        wave_state,
        potential,
        spin_angle,
        magnet,
        magnetic_mask,
        mode_weight,
        source_amp,
        mode_group,
        energies,
        lead_site,
    ):
        sites = wave_state.shape[2]
        dense = (sites // LANES, LANES)
        modes = wave_state.shape[1]
        share = sites // nm
        f32 = jnp.float32
        vmem = pltpu.VMEM
        whole = pl.BlockSpec(memory_space=pl.ANY)
        kept = pl.BlockSpec(memory_space=pltpu.VMEM)
        out = pl.pallas_call(
            functools.partial(kernel, nm, ns, sites),
            out_shape=(
                jax.ShapeDtypeStruct(wave_state.shape, f32),
                jax.ShapeDtypeStruct((5, sites), f32),
                jax.ShapeDtypeStruct((3, sites), f32),
            ),
            in_specs=[whole] * 10,
            out_specs=(kept, kept, kept),
            scratch_shapes=[
                vmem(wave_state.shape, f32),
                vmem(dense, f32),
                vmem(dense, f32),
                vmem((3, sites), f32),
                vmem(dense, jnp.int32),
                vmem((1, modes), f32),
                vmem((4, modes), f32),
                vmem((1, modes), jnp.int32),
                vmem((1, energies.shape[0]), f32),
                vmem((1, modes), jnp.int32),
                vmem(dense, f32),
                vmem(dense, f32),
                vmem(dense, f32),
                vmem(dense, f32),
                vmem(dense, f32),
                vmem((18, modes, LANES), f32),
                vmem((4, modes, sites + 2 * LANES), f32),
                vmem((4, modes, sites + 2 * LANES), f32),
                vmem((4, modes, sites + 2 * LANES), f32),
                vmem((6, modes, sites), f32),
                vmem((2, modes, sites), f32),
                vmem((5, modes, LANES), f32),
                vmem((5, modes, LANES), f32),
                vmem((5, modes, LANES), f32),
                vmem((5, modes, LANES), f32),
                vmem((8, sites), f32),
                vmem((nm - 1, 8, share), f32),
                vmem((8, share), f32),
                vmem((nm, 8, share), f32),
                pltpu.SemaphoreType.DMA((10,)),
                pltpu.SemaphoreType.DMA((2,)),
                pltpu.SemaphoreType.DMA((2,)),
                pltpu.SemaphoreType.DMA,
                pltpu.SemaphoreType.DMA,
                pltpu.SemaphoreType.DMA,
                pltpu.SemaphoreType.DMA,
            ],
            compiler_params=pltpu.CompilerParams(
                collective_id=0,
                has_side_effects=True,
                vmem_limit_bytes=32 * 1024 * 1024,
            ),
        )(
            *[
                pltpu.with_memory_space_constraint(x, pltpu.HBM)
                for x in (
                    wave_state,
                    potential.reshape(dense),
                    spin_angle.reshape(dense),
                    magnet,
                    magnetic_mask.reshape(dense),
                    mode_weight.reshape(1, modes),
                    source_amp,
                    mode_group.reshape(1, modes),
                    energies.reshape(1, -1),
                    lead_site.reshape(1, modes),
                )
            ]
        )
        return pl.pallas_call(
            hand_out,
            out_shape=tuple(jax.ShapeDtypeStruct(x.shape, f32) for x in out),
            in_specs=[kept] * 3,
            out_specs=(whole,) * 3,
            scratch_shapes=[pltpu.SemaphoreType.DMA((3,))],
            compiler_params=pltpu.CompilerParams(vmem_limit_bytes=2 * 1024 * 1024),
        )(*out)

    return jax.shard_map(
        local,
        mesh=mesh,
        in_specs=(
            P(None, "modes", "sites"),
            P("sites"),
            P("sites"),
            P(None, "sites"),
            P("sites"),
            P("modes"),
            P(None, "modes"),
            P("modes"),
            P(),
            P("modes"),
        ),
        out_specs=(P(None, "modes", "sites"), P(None, "sites"), P(None, "sites")),
        check_vma=False,
    )
```

```python
import functools
import math

import jax
import jax.numpy as jnp
from jax import lax
from jax.experimental import pallas as pl
from jax.experimental.pallas import tpu as pltpu
from jax.sharding import PartitionSpec as P

time_step = 0.6
start_time = 10.0
exchange_coupling = 0.5
MESH = pl.DeviceIdType.MESH
LANES = 128
OWNERS = 4

E4 = time_step**4 / 24.0
STAGE_WEIGHT = [
    24.0 / time_step**4,
    24.0 / time_step**3,
    12.0 / time_step**2,
    4.0 / time_step,
]


def apply_stage(y, left, right, coef, base, weight, src, masks):
    ur, dr, ui, di = y
    a_up, a_dn, fx, fy = coef
    near = [l + r for l, r in zip(left, right)]
    h_ur = a_up * ur + fx * dr + fy * di - near[0]
    h_dr = a_dn * dr + fx * ur - fy * ui - near[1]
    h_ui = a_up * ui + fx * di - fy * dr - near[2]
    h_di = a_dn * di + fx * ui + fy * ur - near[3]
    cm, sm = masks
    src_ur = cm * src[0] + sm * src[1]
    src_dr = cm * src[1] - sm * src[0]
    src_ui = cm * src[2] + sm * src[3]
    src_di = cm * src[3] - sm * src[2]
    return [
        (weight * base[0] + src_ur) + h_ui,
        (weight * base[1] + src_dr) + h_di,
        (weight * base[2] + src_ui) - h_ur,
        (weight * base[3] + src_di) - h_dr,
    ]


def kernel(
    nm,
    ns,
    sites,
    wave_hbm,
    pot_hbm,
    ang_hbm,
    mag_hbm,
    mask_hbm,
    wt_hbm,
    amp_hbm,
    grp_hbm,
    en_hbm,
    lead_hbm,
    next_out,
    dens_out,
    magn_out,
    wave,
    pot,
    ang,
    mag,
    mask,
    wt,
    amp,
    grp,
    en,
    lead,
    cos_d,
    sin_d,
    cos2_d,
    sin2_d,
    half_d,
    mag_d,
    mag_n,
    par,
    w,
    ya,
    yb,
    coef,
    cmask,
    edge_l,
    edge_r,
    halo_l,
    halo_r,
    bond_a,
    bond_b,
    slots_a,
    slots_b,
    part,
    slots,
    own,
    sums,
    in_sem,
    halo_send,
    halo_recv,
    a_send,
    a_recv,
    b_send,
    b_recv,
    rs_send,
    rs_recv,
    ag_send,
    ag_recv,
    ready,
):
    chunks = sites // LANES
    owners = min(OWNERS, nm)
    run = chunks // owners
    unroll = 4
    me = lax.axis_index("modes")
    tile = lax.axis_index("sites")
    turn_tile = ns // 2
    has_left = tile > 0
    has_right = tile < ns - 1
    is_owner = me < owners
    keeper = owners - 1
    keeps = me == keeper
    early = tile == turn_tile
    late = tile == turn_tile - 1
    order = [k for k in (1, 2, 3, 4, 5, 6, 7, 12, 13, 14, 15, 8, 9, 10, 11) if k < nm]

    def signal(sem, where):
        pl.semaphore_signal(sem, inc=1, device_id=where, device_id_type=MESH)

    def send(src, dst, send_sem, recv_sem, where):
        return pltpu.make_async_remote_copy(
            src_ref=src,
            dst_ref=dst,
            send_sem=send_sem,
            recv_sem=recv_sem,
            device_id=where,
            device_id_type=MESH,
        )

    barrier = pltpu.get_barrier_semaphore()

    @pl.when(is_owner)
    def _():
        for k in order:
            signal(barrier, {"modes": me ^ k})

    @pl.when(has_right & jnp.logical_not(late))
    def _():
        signal(barrier, {"sites": tile + 1})

    @pl.when(early)
    def _():
        signal(barrier, {"sites": tile - 1})

    @pl.when(keeps & has_right & jnp.logical_not(late))
    def _():
        for m in range(nm):
            signal(barrier, {"modes": jnp.int32(m), "sites": tile + 1})

    fetches = [
        pltpu.make_async_copy(src, dst, in_sem.at[i])
        for i, (src, dst) in enumerate(
            [
                (wt_hbm, wt),
                (amp_hbm, amp),
                (grp_hbm, grp),
                (en_hbm, en),
                (lead_hbm, lead),
                (ang_hbm, ang),
                (pot_hbm, pot),
                (mag_hbm, mag),
                (mask_hbm, mask),
                (wave_hbm, wave),
            ]
        )
    ]
    for fetch in reversed(fetches):
        fetch.start()
    for fetch in fetches[:5]:
        fetch.wait()

    group = grp[...]
    energy_row = en[...]
    energy = jnp.zeros(group.shape, jnp.float32)
    for g in range(energy_row.shape[1]):
        energy = energy + jnp.where(group == g, energy_row[:, g : g + 1], 0.0)
    amp_re = amp[0:2, :]
    amp_im = amp[2:4, :]
    rate = []
    for offset in (0.0, 0.5 * time_step, time_step):
        phase = energy * (start_time + offset)
        cosine = jnp.cos(phase)
        sine = jnp.sin(phase)
        rate.append(
            (
                amp_im * cosine - amp_re * sine,
                -(amp_re * cosine + amp_im * sine),
            )
        )
    mixes = [
        [time_step / 6.0, 4.0 * time_step / 6.0, time_step / 6.0],
        [time_step / 6.0, 2.0 * time_step / 6.0, 0.0],
        [time_step / 6.0, time_step / 6.0, 0.0],
        [time_step / 4.0, 0.0, 0.0],
    ]
    modes = group.shape[1]
    diag = lax.broadcasted_iota(jnp.int32, (modes, modes), 0) == lax.broadcasted_iota(
        jnp.int32, (modes, modes), 1
    )

    def column(row):
        spread = jnp.where(diag, jnp.broadcast_to(row, (modes, modes)), 0.0)
        return jnp.broadcast_to(jnp.sum(spread, axis=1, keepdims=True), (modes, LANES))

    for k in range(4):
        for half in range(2):
            mixed = sum(
                (STAGE_WEIGHT[k] * mixes[k][t]) * rate[t][half]
                for t in range(3)
                if mixes[k][t] != 0.0
            )
            for spin in range(2):
                par[4 * k + 2 * half + spin] = column(mixed[spin : spin + 1, :])
    par[16] = column(wt[...])
    par[17] = column(lead[...].astype(jnp.float32))

    for fetch in fetches[5:9]:
        fetch.wait()
    angle = ang[...]
    cosine = jnp.cos(angle)
    sine = jnp.sin(angle)
    cos_d[...] = cosine
    sin_d[...] = sine
    cos2_d[...] = 1.0 - 2.0 * sine * sine
    sin2_d[...] = 2.0 * sine * cosine
    half_d[...] = exchange_coupling * mask[...].astype(jnp.float32)

    zero = jnp.zeros((8, LANES), jnp.float32)
    for buf in (w, ya, yb):
        for c in range(4):
            buf[c, :, 0:LANES] = zero
            buf[c, :, LANES + sites : 2 * LANES + sites] = zero
    lane = lax.broadcasted_iota(jnp.int32, (8, LANES), 1)
    sub = lax.broadcasted_iota(jnp.int32, (8, LANES), 0)
    first = lane == 0
    last = lane == LANES - 1
    span = float(sites * ns // 8)

    def in_region(position):
        away = position.astype(jnp.float32) - par[17]
        return (away >= 0.0) & (away < span)

    def row(ref, i):
        return jnp.broadcast_to(ref[pl.ds(i, 1), :], (8, LANES))

    fetches[9].wait()

    def at(c, shift=0):
        return pl.ds(pl.multiple_of(c * LANES, LANES) + shift * LANES, LANES)

    def rotate(block, carry):
        for u in range(unroll):
            c = block * unroll + u
            cs = row(cos_d, c)
            sn = row(sin_d, c)
            c2 = row(cos2_d, c)
            s2 = row(sin2_d, c)
            half = row(half_d, c)
            field = [half * jnp.broadcast_to(mag[i : i + 1, at(c)], (8, LANES)) for i in range(3)]
            v = row(pot, c)
            fz = c2 * field[2] + s2 * field[0]
            coef[0, :, at(c)] = v + fz
            coef[1, :, at(c)] = v - fz
            coef[2, :, at(c)] = c2 * field[0] - s2 * field[2]
            coef[3, :, at(c)] = field[1]
            coef[4, :, at(c)] = cs
            coef[5, :, at(c)] = sn
            inside = in_region(tile * sites + c * LANES + lane)
            cmask[0, :, at(c)] = jnp.where(inside, cs, 0.0)
            cmask[1, :, at(c)] = jnp.where(inside, sn, 0.0)
            for part_i in range(2):
                up = wave[2 * part_i, :, at(c)]
                down = wave[2 * part_i + 1, :, at(c)]
                w[2 * part_i, :, at(c, 1)] = cs * up + sn * down
                w[2 * part_i + 1, :, at(c, 1)] = cs * down - sn * up
        return carry

    lax.fori_loop(0, chunks // unroll, rotate, 0)

    all_modes = float(modes * nm)
    root = 1.0 / math.sqrt(all_modes)
    weight = par[16]

    for edge, c in ((edge_l, 0), (edge_r, chunks - 1)):
        for i in range(4):
            edge[i] = w[i, :, (c + 1) * LANES : (c + 2) * LANES]
        rows = zero
        for i in range(6):
            rows = jnp.where(sub == i, coef[i, :, c * LANES : (c + 1) * LANES], rows)
        edge[4] = rows
    left_factor = zero
    right_factor = zero
    for i in range(4):
        left_factor = jnp.where(lane == i, pltpu.roll(edge_r[i], 1 + i, 1), left_factor)
        other = edge_l[(i + 2) % 4]
        other = pltpu.roll(other, i, 1) if i else other
        right_factor = jnp.where(lane == i, other if i < 2 else -other, right_factor)
    bond_a[...] = (2.0 * root) * (weight * left_factor)
    bond_b[...] = right_factor

    to_left = send(
        edge_l, halo_r, halo_send.at[0], halo_recv.at[0], {"sites": jnp.maximum(tile - 1, 0)}
    )
    to_right = send(
        edge_r, halo_l, halo_send.at[1], halo_recv.at[1], {"sites": jnp.minimum(tile + 1, ns - 1)}
    )
    to_keeper = send(bond_a, slots_a.at[me], a_send, a_recv, {"modes": jnp.int32(keeper)})
    to_left_keeper = send(
        bond_b,
        slots_b.at[me],
        b_send,
        b_recv,
        {"modes": jnp.int32(keeper), "sites": jnp.maximum(tile - 1, 0)},
    )

    pl.semaphore_wait(
        barrier,
        owners
        - is_owner.astype(jnp.int32)
        + 2 * (has_left & jnp.logical_not(early)).astype(jnp.int32)
        + late.astype(jnp.int32),
    )

    @pl.when(late)
    def _():
        signal(ready, {"sites": tile + 1})
        to_right.start()

    @pl.when(has_left & jnp.logical_not(early))
    def _():
        to_left_keeper.start()
        to_left.start()

    @pl.when(jnp.logical_not(keeps))
    def _():
        to_keeper.start()

    def current(wc, wn, weight):
        after = [jnp.where(first, n, c) for c, n in zip(wc, wn)]
        after = [pltpu.roll(a, LANES - 1, 1) for a in after]
        return weight * (
            wc[0] * after[2] - wc[2] * after[0] + (wc[1] * after[3] - wc[3] * after[1])
        )

    def down_sum(x):
        return jnp.sum(x, axis=0, keepdims=True)

    run_sub = lax.broadcasted_iota(jnp.int32, (run, LANES), 0)

    def density(block, carry):
        q = lax.rem(block + me, owners)
        wc = [w[i, :, at(q * run, 1)] for i in range(4)]
        packed = [jnp.zeros((run, LANES), jnp.float32) for _ in range(5)]
        for u in range(run):
            c = q * run + u
            wn = [w[i, :, at(c, 2)] for i in range(4)]
            ur, dr, ui, di = [wave[i, :, at(c)] for i in range(4)]
            wur, wdr, wui, wdi = [weight * x for x in (ur, dr, ui, di)]
            up = down_sum(wur * ur + wui * ui)
            dn = down_sum(wdr * dr + wdi * di)
            sx = down_sum(wur * dr + wui * di)
            sy = down_sum(wur * di - wui * dr)
            cur = down_sum(current(wc, wn, weight))
            for i, r in enumerate([up, sx, sy, dn, cur]):
                packed[i] = jnp.where(run_sub == u, jnp.broadcast_to(r, (run, LANES)), packed[i])
            wc = wn
        up, sx, sy, dn, cur = packed
        rows = [
            (up + dn) * (1.0 / all_modes),
            sx * (2.0 * root),
            sy * (2.0 * root),
            (up - dn) * root,
            cur * (2.0 * root),
        ]
        for i, r in enumerate(rows):
            part[q, i * run : (i + 1) * run, :] = r

        @pl.when(q != me)
        def _():
            send(part.at[q], slots.at[me], rs_send.at[q], rs_recv, {"modes": q}).start()

        return carry

    lax.fori_loop(0, owners, density, 0)

    def stage_pass(src_ref, dst_ref, k):
        def body(block, carry):
            def load(c, shift):
                return [src_ref[i, :, at(c, shift)] for i in range(4)]

            c0 = block * unroll
            prev = load(c0, 0)
            here = load(c0, 1)
            for u in range(unroll):
                c = c0 + u
                after = load(c, 2)
                lefts = [pltpu.roll(jnp.where(last, p, h), 1, 1) for p, h in zip(prev, here)]
                rights = [
                    pltpu.roll(jnp.where(first, a, h), LANES - 1, 1) for a, h in zip(after, here)
                ]
                base = here if k == 3 else [w[i, :, at(c, 1)] for i in range(4)]
                out = apply_stage(
                    here,
                    lefts,
                    rights,
                    [coef[i, :, at(c)] for i in range(4)],
                    base,
                    STAGE_WEIGHT[k],
                    [par[4 * k + i] for i in range(4)],
                    [cmask[0, :, at(c)], cmask[1, :, at(c)]],
                )
                if k > 0:
                    for i in range(4):
                        dst_ref[i, :, at(c, 1)] = out[i]
                else:
                    cs = E4 * coef[4, :, at(c)]
                    sn = E4 * coef[5, :, at(c)]
                    for h in range(2):
                        next_out[2 * h, :, at(c)] = cs * out[2 * h] - sn * out[2 * h + 1]
                        next_out[2 * h + 1, :, at(c)] = sn * out[2 * h] + cs * out[2 * h + 1]
                prev, here = here, after
            return carry

        lax.fori_loop(0, chunks // unroll, body, 0)

    stage_pass(w, ya, 3)
    stage_pass(ya, yb, 2)
    stage_pass(yb, ya, 1)

    @pl.when(has_right & jnp.logical_not(late))
    def _():
        to_left.wait_recv()
        to_right.start()

    @pl.when(is_owner)
    def _():
        pltpu.make_async_copy(
            slots.at[0 : nm - 1], slots.at[0 : nm - 1], rs_recv
        ).wait()
        total = part[me]
        for k in range(1, nm):
            total = total + slots[me ^ k]
        own[...] = total

        @pl.when(keeps)
        def _():
            pltpu.make_async_copy(
                slots_a.at[0 : nm - 1], slots_a.at[0 : nm - 1], a_recv
            ).wait()

        @pl.when(keeps & has_right)
        def _():
            pltpu.make_async_copy(slots_b, slots_b, b_recv).wait()
            bond = bond_a[...] * slots_b[keeper]
            for m in range(nm):
                if m != keeper:
                    bond = bond + slots_a[m] * slots_b[m]
            bond = jnp.sum(down_sum(bond), axis=1, keepdims=True)
            spot = (run_sub[0:1] == 0) & last[0:1]
            end = 5 * run - 1
            own[end : end + 1, :] = own[end : end + 1, :] + jnp.where(
                spot, jnp.broadcast_to(bond, (1, LANES)), 0.0
            )

        for k in order:
            send(own, sums.at[me], ag_send, ag_recv.at[me], {"modes": me ^ k}).start()
        sums[me] = own[...]

    stage_pass(ya, None, 0)
    for i in range(3):
        for c in range(chunks):
            mag_d[i, c : c + 1, :] = mag[i : i + 1, c * LANES : (c + 1) * LANES]

    def redo_ends():
        @pl.when(has_left)
        def _():
            to_right.wait_recv()

        @pl.when(late)
        def _():
            to_left.wait_recv()

        base = []
        coefs = []
        masks = []
        alive = []
        for where in range(4):
            if where in (0, 3):
                halo = halo_l if where == 0 else halo_r
                there = has_left if where == 0 else has_right
                keep = jnp.full((8, LANES), there.astype(jnp.int32)) > 0
                alive.append(keep)
                base.append([jnp.where(keep, halo[i], 0.0) for i in range(4)])
                rows = [jnp.broadcast_to(halo[4, i : i + 1, :], (8, LANES)) for i in range(6)]
                coefs.append(rows[:4])
                start = tile * sites + (-LANES if where == 0 else sites)
                inside = in_region(start + lane)
                masks.append([jnp.where(inside, rows[4], 0.0), jnp.where(inside, rows[5], 0.0)])
            else:
                c = 0 if where == 1 else chunks - 1
                cut = slice(c * LANES, (c + 1) * LANES)
                alive.append(None)
                base.append([w[i, :, (c + 1) * LANES : (c + 2) * LANES] for i in range(4)])
                coefs.append([coef[i, :, cut] for i in range(4)])
                masks.append([cmask[0, :, cut], cmask[1, :, cut]])
        y = base
        for k in (3, 2, 1, 0):
            out = []
            for where in range(4):
                prev, here, after = y[(where + 3) % 4], y[where], y[(where + 1) % 4]
                lefts = [pltpu.roll(jnp.where(last, p, h), 1, 1) for p, h in zip(prev, here)]
                rights = [
                    pltpu.roll(jnp.where(first, a, h), LANES - 1, 1) for a, h in zip(after, here)
                ]
                new = apply_stage(
                    here,
                    lefts,
                    rights,
                    coefs[where],
                    base[where],
                    STAGE_WEIGHT[k],
                    [par[4 * k + i] for i in range(4)],
                    masks[where],
                )
                if alive[where] is not None:
                    new = [jnp.where(alive[where], x, 0.0) for x in new]
                out.append(new)
            y = out
        for where, c in ((1, 0), (2, chunks - 1)):
            cut = slice(c * LANES, (c + 1) * LANES)
            cs = E4 * coef[4, :, cut]
            sn = E4 * coef[5, :, cut]
            fresh = lane < 4 if where == 1 else lane >= LANES - 4
            for h in range(2):
                up = cs * y[where][2 * h] - sn * y[where][2 * h + 1]
                down = sn * y[where][2 * h] + cs * y[where][2 * h + 1]
                next_out[2 * h, :, cut] = jnp.where(fresh, up, next_out[2 * h, :, cut])
                next_out[2 * h + 1, :, cut] = jnp.where(fresh, down, next_out[2 * h + 1, :, cut])

    @pl.when(jnp.logical_not(early))
    def _():
        redo_ends()

    @pl.when(early)
    def _():
        pl.semaphore_wait(ready, 1)
        to_left_keeper.start()
        to_left.start()

    for q in range(owners):
        @pl.when(me != q)
        def _():
            pltpu.make_async_copy(own, sums.at[q], ag_recv.at[q]).wait()

        hx, hy, hz = [sums[q, i * run : (i + 1) * run, :] for i in (1, 2, 3)]
        m = [mag_d[i, q * run : (q + 1) * run, :] for i in range(3)]
        turn = time_step * half_d[q * run : (q + 1) * run, :]
        mag_n[0:run, :] = m[0] - turn * (m[1] * hz - m[2] * hy)
        mag_n[run : 2 * run, :] = m[1] - turn * (m[2] * hx - m[0] * hz)
        mag_n[2 * run : 3 * run, :] = m[2] - turn * (m[0] * hy - m[1] * hx)
        for u in range(run):
            cut = slice((q * run + u) * LANES, (q * run + u + 1) * LANES)
            dens_out[:, cut] = sums[q, pl.ds(u, 5, stride=run), :]
            magn_out[:, cut] = mag_n[pl.ds(u, 3, stride=run), :]

    @pl.when(early)
    def _():
        redo_ends()

    @pl.when(has_right)
    def _():
        to_right.wait_send()

    @pl.when(has_left)
    def _():
        to_left.wait_send()
        to_left_keeper.wait_send()

    @pl.when(jnp.logical_not(keeps))
    def _():
        to_keeper.wait_send()

    for q in range(owners):
        @pl.when(me != q)
        def _():
            pltpu.make_async_copy(own, own, rs_send.at[q]).wait()

    @pl.when(is_owner)
    def _():
        pltpu.make_async_copy(slots.at[0 : nm - 1], slots.at[0 : nm - 1], ag_send).wait()


def hand_out(next_v, dens_v, magn_v, next_out, dens_out, magn_out, sem):
    copies = [
        pltpu.make_async_copy(src, dst, sem.at[i])
        for i, (src, dst) in enumerate(
            [(next_v, next_out), (dens_v, dens_out), (magn_v, magn_out)]
        )
    ]
    for copy in copies:
        copy.start()
    for copy in copies:
        copy.wait()


def solution(mesh):
    nm = mesh.shape["modes"]
    ns = mesh.shape["sites"]

    def local(
        wave_state,
        potential,
        spin_angle,
        magnet,
        magnetic_mask,
        mode_weight,
        source_amp,
        mode_group,
        energies,
        lead_site,
    ):
        sites = wave_state.shape[2]
        dense = (sites // LANES, LANES)
        modes = wave_state.shape[1]
        owners = min(OWNERS, nm)
        rows = 5 * dense[0] // owners
        f32 = jnp.float32
        vmem = pltpu.VMEM
        whole = pl.BlockSpec(memory_space=pl.ANY)
        kept = pl.BlockSpec(memory_space=pltpu.VMEM)
        out = pl.pallas_call(
            functools.partial(kernel, nm, ns, sites),
            out_shape=(
                jax.ShapeDtypeStruct(wave_state.shape, f32),
                jax.ShapeDtypeStruct((5, sites), f32),
                jax.ShapeDtypeStruct((3, sites), f32),
            ),
            in_specs=[whole] * 10,
            out_specs=(kept, kept, kept),
            scratch_shapes=[
                vmem(wave_state.shape, f32),
                vmem(dense, f32),
                vmem(dense, f32),
                vmem((3, sites), f32),
                vmem(dense, jnp.int32),
                vmem((1, modes), f32),
                vmem((4, modes), f32),
                vmem((1, modes), jnp.int32),
                vmem((1, energies.shape[0]), f32),
                vmem((1, modes), jnp.int32),
                vmem(dense, f32),
                vmem(dense, f32),
                vmem(dense, f32),
                vmem(dense, f32),
                vmem(dense, f32),
                vmem((3, *dense), f32),
                vmem((3 * rows // 5, LANES), f32),
                vmem((18, modes, LANES), f32),
                vmem((4, modes, sites + 2 * LANES), f32),
                vmem((4, modes, sites + 2 * LANES), f32),
                vmem((4, modes, sites + 2 * LANES), f32),
                vmem((6, modes, sites), f32),
                vmem((2, modes, sites), f32),
                vmem((5, modes, LANES), f32),
                vmem((5, modes, LANES), f32),
                vmem((5, modes, LANES), f32),
                vmem((5, modes, LANES), f32),
                vmem((modes, LANES), f32),
                vmem((modes, LANES), f32),
                vmem((nm, modes, LANES), f32),
                vmem((nm, modes, LANES), f32),
                vmem((owners, rows, LANES), f32),
                vmem((nm, rows, LANES), f32),
                vmem((rows, LANES), f32),
                vmem((owners, rows, LANES), f32),
                pltpu.SemaphoreType.DMA((10,)),
                pltpu.SemaphoreType.DMA((2,)),
                pltpu.SemaphoreType.DMA((2,)),
                pltpu.SemaphoreType.DMA,
                pltpu.SemaphoreType.DMA,
                pltpu.SemaphoreType.DMA,
                pltpu.SemaphoreType.DMA,
                pltpu.SemaphoreType.DMA((owners,)),
                pltpu.SemaphoreType.DMA,
                pltpu.SemaphoreType.DMA,
                pltpu.SemaphoreType.DMA((owners,)),
                pltpu.SemaphoreType.REGULAR,
            ],
            compiler_params=pltpu.CompilerParams(
                collective_id=0,
                has_side_effects=True,
                vmem_limit_bytes=32 * 1024 * 1024,
            ),
        )(
            *[
                pltpu.with_memory_space_constraint(x, pltpu.HBM)
                for x in (
                    wave_state,
                    potential.reshape(dense),
                    spin_angle.reshape(dense),
                    magnet,
                    magnetic_mask.reshape(dense),
                    mode_weight.reshape(1, modes),
                    source_amp,
                    mode_group.reshape(1, modes),
                    energies.reshape(1, -1),
                    lead_site.reshape(1, modes),
                )
            ]
        )
        return pl.pallas_call(
            hand_out,
            out_shape=tuple(jax.ShapeDtypeStruct(x.shape, f32) for x in out),
            in_specs=[kept] * 3,
            out_specs=(whole,) * 3,
            scratch_shapes=[pltpu.SemaphoreType.DMA((3,))],
            compiler_params=pltpu.CompilerParams(vmem_limit_bytes=2 * 1024 * 1024),
        )(*out)

    return jax.shard_map(
        local,
        mesh=mesh,
        in_specs=(
            P(None, "modes", "sites"),
            P("sites"),
            P("sites"),
            P(None, "sites"),
            P("sites"),
            P("modes"),
            P(None, "modes"),
            P("modes"),
            P(),
            P("modes"),
        ),
        out_specs=(P(None, "modes", "sites"), P(None, "sites"), P(None, "sites")),
        check_vma=False,
    )
```

```python
import functools
import math

import jax
import jax.numpy as jnp
from jax import lax
from jax.experimental import pallas as pl
from jax.experimental.pallas import tpu as pltpu
from jax.sharding import PartitionSpec as P

time_step = 0.6
start_time = 10.0
exchange_coupling = 0.5
MESH = pl.DeviceIdType.MESH
LANES = 128
SHARES = 8
FIRST_TILE_OWNERS = {16: (1, 1, 2, 3, 4, 5, 12, 13), 4: (1, 1, 1, 1, 2, 2, 3, 3)}

E4 = time_step**4 / 24.0
STAGE_WEIGHT = [
    24.0 / time_step**4,
    24.0 / time_step**3,
    12.0 / time_step**2,
    4.0 / time_step,
]


def apply_stage(y, left, right, coef, base, weight, src, masks):
    ur, dr, ui, di = y
    a_up, a_dn, fx, fy = coef
    near = [l + r for l, r in zip(left, right)]
    h_ur = a_up * ur + fx * dr + fy * di - near[0]
    h_dr = a_dn * dr + fx * ur - fy * ui - near[1]
    h_ui = a_up * ui + fx * di - fy * dr - near[2]
    h_di = a_dn * di + fx * ui + fy * ur - near[3]
    cm, sm = masks
    src_ur = cm * src[0] + sm * src[1]
    src_dr = cm * src[1] - sm * src[0]
    src_ui = cm * src[2] + sm * src[3]
    src_di = cm * src[3] - sm * src[2]
    return [
        (weight * base[0] + src_ur) + h_ui,
        (weight * base[1] + src_dr) + h_di,
        (weight * base[2] + src_ui) - h_ur,
        (weight * base[3] + src_di) - h_dr,
    ]


def kernel(
    nm,
    ns,
    sites,
    wave_hbm,
    pot_hbm,
    ang_hbm,
    mag_hbm,
    mask_hbm,
    wt_hbm,
    amp_hbm,
    grp_hbm,
    en_hbm,
    lead_hbm,
    next_out,
    dens_out,
    magn_out,
    wave,
    pot,
    ang,
    mag,
    mask,
    wt,
    amp,
    grp,
    en,
    lead,
    cos_d,
    sin_d,
    cos2_d,
    sin2_d,
    half_d,
    mag_d,
    mag_n,
    par,
    w,
    ya,
    yb,
    coef,
    cmask,
    edge_l,
    edge_r,
    halo_l,
    halo_r,
    bond_a,
    bond_b,
    slots_a,
    slots_b,
    part,
    slots,
    sums,
    in_sem,
    wave_sem,
    halo_send,
    halo_recv,
    a_send,
    a_recv,
    b_send,
    b_recv,
    rs_send,
    rs_recv,
    ag_send,
    ag_recv,
    ready,
):
    chunks = sites // LANES
    run = chunks // SHARES
    unroll = 4
    me = lax.axis_index("modes")
    tile = lax.axis_index("sites")
    turn_tile = ns // 2
    has_left = tile > 0
    has_right = tile < ns - 1
    early = tile == turn_tile
    late = tile == turn_tile - 1
    usual = [q * min(nm, SHARES) // SHARES for q in range(SHARES)]
    special = FIRST_TILE_OWNERS.get(nm, usual)

    def owner_of(q):
        return jnp.where(tile == 0, jnp.int32(special[q]), jnp.int32(usual[q]))

    def owner_at(q):
        found = owner_of(0)
        for i in range(1, SHARES):
            found = jnp.where(q == i, owner_of(i), found)
        return found

    def among(devices):
        found = me == devices[0]
        for d in devices[1:]:
            found = found | (me == d)
        return found

    is_owner = jnp.where(tile == 0, among(sorted(set(special))).astype(jnp.int32), among(sorted(set(usual))).astype(jnp.int32))
    owner_count = jnp.where(tile == 0, len(set(special)), len(set(usual)))
    keeper = owner_of(SHARES - 1)
    keeps = me == keeper
    left_keeper = jnp.where(tile == 1, jnp.int32(special[-1]), jnp.int32(usual[-1]))
    order = [j for j in (1, 3, 0, 2, 5, 7, 4, 6, 9, 11, 8, 10, 13, 15, 12, 14) if j < nm]

    def signal(sem, where):
        pl.semaphore_signal(sem, inc=1, device_id=where, device_id_type=MESH)

    def send(src, dst, send_sem, recv_sem, where):
        return pltpu.make_async_remote_copy(
            src_ref=src,
            dst_ref=dst,
            send_sem=send_sem,
            recv_sem=recv_sem,
            device_id=where,
            device_id_type=MESH,
        )

    barrier = pltpu.get_barrier_semaphore()

    @pl.when(is_owner == 1)
    def _():
        for k in range(1, nm):
            signal(barrier, {"modes": me ^ k})

    @pl.when(has_right & jnp.logical_not(late))
    def _():
        signal(barrier, {"sites": tile + 1})

    @pl.when(early)
    def _():
        signal(barrier, {"sites": tile - 1})

    @pl.when(keeps & has_right & jnp.logical_not(late))
    def _():
        for m in range(nm):
            signal(barrier, {"modes": jnp.int32(m), "sites": tile + 1})

    fetches = [
        pltpu.make_async_copy(src, dst, in_sem.at[i])
        for i, (src, dst) in enumerate(
            [
                (wt_hbm, wt),
                (amp_hbm, amp),
                (grp_hbm, grp),
                (en_hbm, en),
                (lead_hbm, lead),
                (ang_hbm, ang),
                (pot_hbm, pot),
                (mag_hbm, mag),
                (mask_hbm, mask),
            ]
        )
    ]

    def piece(q):
        cut = pl.ds(pl.multiple_of(q * (run * LANES), LANES), run * LANES)
        return pltpu.make_async_copy(
            wave_hbm.at[:, :, cut], wave.at[:, :, cut], wave_sem.at[q]
        )

    for fetch in fetches:
        fetch.start()
    for q in (0, SHARES - 1, *range(1, SHARES - 1)):
        piece(q).start()
    for fetch in fetches[:5]:
        fetch.wait()

    group = grp[...]
    energy_row = en[...]
    energy = jnp.zeros(group.shape, jnp.float32)
    for g in range(energy_row.shape[1]):
        energy = energy + jnp.where(group == g, energy_row[:, g : g + 1], 0.0)
    amp_re = amp[0:2, :]
    amp_im = amp[2:4, :]
    rate = []
    for offset in (0.0, 0.5 * time_step, time_step):
        phase = energy * (start_time + offset)
        cosine = jnp.cos(phase)
        sine = jnp.sin(phase)
        rate.append(
            (
                amp_im * cosine - amp_re * sine,
                -(amp_re * cosine + amp_im * sine),
            )
        )
    mixes = [
        [time_step / 6.0, 4.0 * time_step / 6.0, time_step / 6.0],
        [time_step / 6.0, 2.0 * time_step / 6.0, 0.0],
        [time_step / 6.0, time_step / 6.0, 0.0],
        [time_step / 4.0, 0.0, 0.0],
    ]
    modes = group.shape[1]
    diag = lax.broadcasted_iota(jnp.int32, (modes, modes), 0) == lax.broadcasted_iota(
        jnp.int32, (modes, modes), 1
    )

    def column(row):
        spread = jnp.where(diag, jnp.broadcast_to(row, (modes, modes)), 0.0)
        return jnp.broadcast_to(jnp.sum(spread, axis=1, keepdims=True), (modes, LANES))

    for k in range(4):
        for half in range(2):
            mixed = sum(
                (STAGE_WEIGHT[k] * mixes[k][t]) * rate[t][half]
                for t in range(3)
                if mixes[k][t] != 0.0
            )
            for spin in range(2):
                par[4 * k + 2 * half + spin] = column(mixed[spin : spin + 1, :])
    par[16] = column(wt[...])
    par[17] = column(lead[...].astype(jnp.float32))

    for fetch in fetches[5:9]:
        fetch.wait()
    angle = ang[...]
    cosine = jnp.cos(angle)
    sine = jnp.sin(angle)
    cos_d[...] = cosine
    sin_d[...] = sine
    cos2_d[...] = 1.0 - 2.0 * sine * sine
    sin2_d[...] = 2.0 * sine * cosine
    half_d[...] = exchange_coupling * mask[...].astype(jnp.float32)

    zero = jnp.zeros((8, LANES), jnp.float32)
    for buf in (w, ya, yb):
        for c in range(4):
            buf[c, :, 0:LANES] = zero
            buf[c, :, LANES + sites : 2 * LANES + sites] = zero
    lane = lax.broadcasted_iota(jnp.int32, (8, LANES), 1)
    sub = lax.broadcasted_iota(jnp.int32, (8, LANES), 0)
    first = lane == 0
    last = lane == LANES - 1
    span = float(sites * ns // 8)

    def in_region(position):
        away = position.astype(jnp.float32) - par[17]
        return (away >= 0.0) & (away < span)

    def row(ref, i):
        return jnp.broadcast_to(ref[pl.ds(i, 1), :], (8, LANES))

    def at(c, shift=0):
        return pl.ds(pl.multiple_of(c * LANES, LANES) + shift * LANES, LANES)

    def rotate(q):
        piece(q).wait()
        for u in range(run):
            c = q * run + u
            cs = row(cos_d, c)
            sn = row(sin_d, c)
            c2 = row(cos2_d, c)
            s2 = row(sin2_d, c)
            half = row(half_d, c)
            field = [half * jnp.broadcast_to(mag[i : i + 1, at(c)], (8, LANES)) for i in range(3)]
            v = row(pot, c)
            fz = c2 * field[2] + s2 * field[0]
            coef[0, :, at(c)] = v + fz
            coef[1, :, at(c)] = v - fz
            coef[2, :, at(c)] = c2 * field[0] - s2 * field[2]
            coef[3, :, at(c)] = field[1]
            coef[4, :, at(c)] = cs
            coef[5, :, at(c)] = sn
            inside = in_region(tile * sites + c * LANES + lane)
            cmask[0, :, at(c)] = jnp.where(inside, cs, 0.0)
            cmask[1, :, at(c)] = jnp.where(inside, sn, 0.0)
            for part_i in range(2):
                up = wave[2 * part_i, :, at(c)]
                down = wave[2 * part_i + 1, :, at(c)]
                w[2 * part_i, :, at(c, 1)] = cs * up + sn * down
                w[2 * part_i + 1, :, at(c, 1)] = cs * down - sn * up

    pl.semaphore_wait(
        barrier,
        owner_count
        - is_owner
        + 2 * (has_left & jnp.logical_not(early)).astype(jnp.int32)
        + late.astype(jnp.int32),
    )

    @pl.when(late)
    def _():
        signal(ready, {"sites": tile + 1})

    rotate(0)
    rotate(SHARES - 1)

    all_modes = float(modes * nm)
    root = 1.0 / math.sqrt(all_modes)
    weight = root * par[16]

    for edge, c in ((edge_l, 0), (edge_r, chunks - 1)):
        for i in range(4):
            edge[i] = w[i, :, (c + 1) * LANES : (c + 2) * LANES]
        rows = zero
        for i in range(6):
            rows = jnp.where(sub == i, coef[i, :, c * LANES : (c + 1) * LANES], rows)
        edge[4] = rows
    left_factor = zero
    right_factor = zero
    for i in range(4):
        left_factor = jnp.where(lane == i, pltpu.roll(edge_r[i], 1 + i, 1), left_factor)
        other = edge_l[(i + 2) % 4]
        other = pltpu.roll(other, i, 1) if i else other
        right_factor = jnp.where(lane == i, other if i < 2 else -other, right_factor)
    bond_a[...] = 2.0 * (weight * left_factor)
    bond_b[...] = right_factor

    to_left = send(
        edge_l, halo_r, halo_send.at[0], halo_recv.at[0], {"sites": jnp.maximum(tile - 1, 0)}
    )
    to_right = send(
        edge_r, halo_l, halo_send.at[1], halo_recv.at[1], {"sites": jnp.minimum(tile + 1, ns - 1)}
    )
    to_keeper = send(bond_a, slots_a.at[me], a_send, a_recv, {"modes": keeper})
    to_left_keeper = send(
        bond_b,
        slots_b.at[me],
        b_send,
        b_recv,
        {"modes": left_keeper, "sites": jnp.maximum(tile - 1, 0)},
    )

    @pl.when(late)
    def _():
        to_right.start()

    @pl.when(has_left & jnp.logical_not(early))
    def _():
        to_left_keeper.start()
        to_left.start()

    @pl.when(jnp.logical_not(keeps))
    def _():
        to_keeper.start()

    def current(wc, wn, weight):
        after = [jnp.where(first, n, c) for c, n in zip(wc, wn)]
        after = [pltpu.roll(a, LANES - 1, 1) for a in after]
        return weight * (
            wc[0] * after[2] - wc[2] * after[0] + (wc[1] * after[3] - wc[3] * after[1])
        )

    def down_sum(x):
        return jnp.sum(x, axis=0, keepdims=True)

    odd = (sub & 1) == 1
    upper_pair = (sub & 2) == 2
    lower_half = sub < 4

    def fold(x, y, other, shift):
        return jnp.where(other, y, x) + pltpu.roll(jnp.where(other, x, y), 8 - shift, 0)

    def fold_four(x):
        return fold(fold(x[0], x[1], odd, 1), fold(x[2], x[3], odd, 1), upper_pair, 2)

    def fold_eight(x):
        return fold(fold_four(x[:4]), fold_four(x[4:]), jnp.logical_not(lower_half), 4)

    first_scale = jnp.where(lower_half, root, 2.0)
    second_scale = jnp.where(lower_half, 2.0, 1.0)

    def density(q):
        wc = [w[i, :, at(q * run, 1)] for i in range(4)]
        tiles = [[], [], [], [], []]
        for u in range(run):
            c = q * run + u
            wn = [w[i, :, at(c, 2)] for i in range(4)]
            ur, dr, ui, di = [wave[i, :, at(c)] for i in range(4)]
            wur, wdr, wui, wdi = [weight * x for x in (ur, dr, ui, di)]
            up = wur * ur + wui * ui
            dn = wdr * dr + wdi * di
            tiles[0].append(up + dn)
            tiles[1].append(wur * dr + wui * di)
            tiles[2].append(wur * di - wui * dr)
            tiles[3].append(up - dn)
            tiles[4].append(current(wc, wn, weight))
            wc = wn
        part[q, 0:8, :] = first_scale * fold_eight(tiles[0] + tiles[1])
        part[q, 8:16, :] = second_scale * fold_eight(tiles[2] + tiles[3])
        bonds = fold_four(tiles[4])
        part[q, 16:20, :] = (2.0 * (bonds + pltpu.roll(bonds, 4, 0)))[0:4, :]
        owner = owner_at(q)

        @pl.when(owner != me)
        def _():
            send(part.at[q], slots.at[q, me], rs_send.at[q], rs_recv.at[q], {"modes": owner}).start()

    def stream(q, carry):
        rotate(q)
        density(q - 1)
        return carry

    def finish(q, carry):
        density(q)
        return carry

    lax.fori_loop(1, SHARES - 1, stream, 0)
    lax.fori_loop(SHARES - 2, SHARES, finish, 0)

    def stage_pass(src_ref, dst_ref, k):
        def body(block, carry):
            def load(c, shift):
                return [src_ref[i, :, at(c, shift)] for i in range(4)]

            c0 = block * unroll
            prev = load(c0, 0)
            here = load(c0, 1)
            for u in range(unroll):
                c = c0 + u
                after = load(c, 2)
                lefts = [pltpu.roll(jnp.where(last, p, h), 1, 1) for p, h in zip(prev, here)]
                rights = [
                    pltpu.roll(jnp.where(first, a, h), LANES - 1, 1) for a, h in zip(after, here)
                ]
                base = here if k == 3 else [w[i, :, at(c, 1)] for i in range(4)]
                out = apply_stage(
                    here,
                    lefts,
                    rights,
                    [coef[i, :, at(c)] for i in range(4)],
                    base,
                    STAGE_WEIGHT[k],
                    [par[4 * k + i] for i in range(4)],
                    [cmask[0, :, at(c)], cmask[1, :, at(c)]],
                )
                if k > 0:
                    for i in range(4):
                        dst_ref[i, :, at(c, 1)] = out[i]
                else:
                    cs = E4 * coef[4, :, at(c)]
                    sn = E4 * coef[5, :, at(c)]
                    for h in range(2):
                        next_out[2 * h, :, at(c)] = cs * out[2 * h] - sn * out[2 * h + 1]
                        next_out[2 * h + 1, :, at(c)] = sn * out[2 * h] + cs * out[2 * h + 1]
                prev, here = here, after
            return carry

        lax.fori_loop(0, chunks // unroll, body, 0)

    stage_pass(w, ya, 3)
    stage_pass(ya, yb, 2)
    stage_pass(yb, ya, 1)

    @pl.when(has_right & jnp.logical_not(late))
    def _():
        to_left.wait_recv()
        to_right.start()

    def add_up(q, carry):
        @pl.when(owner_at(q) == me)
        def _():
            pltpu.make_async_copy(
                slots.at[q, 0 : nm - 1], slots.at[q, 0 : nm - 1], rs_recv.at[q]
            ).wait()
            total = part[q]
            for k in range(1, nm):
                total = total + slots[q, me ^ k]
            sums[q] = total

            @pl.when(q == SHARES - 1)
            def _():
                pltpu.make_async_copy(
                    slots_a.at[0 : nm - 1], slots_a.at[0 : nm - 1], a_recv
                ).wait()

            @pl.when((q == SHARES - 1) & has_right)
            def _():
                pltpu.make_async_copy(slots_b, slots_b, b_recv).wait()
                bond = bond_a[...] * slots_b[me]
                for k in range(1, nm):
                    bond = bond + slots_a[me ^ k] * slots_b[me ^ k]
                bond = jnp.sum(down_sum(bond), axis=1, keepdims=True)
                end = 5 * run - 1
                sums[q, end : end + 1, :] = sums[q, end : end + 1, :] + jnp.where(
                    last[0:1], jnp.broadcast_to(bond, (1, LANES)), 0.0
                )

            for j in order:
                @pl.when(me != j)
                def _():
                    send(
                        sums.at[q],
                        sums.at[q],
                        ag_send.at[q],
                        ag_recv.at[q],
                        {"modes": jnp.int32(j)},
                    ).start()

        return carry

    lax.fori_loop(0, SHARES, add_up, 0)

    stage_pass(ya, None, 0)
    for i in range(3):
        for c in range(chunks):
            mag_d[i, c : c + 1, :] = mag[i : i + 1, c * LANES : (c + 1) * LANES]

    def redo_ends():
        @pl.when(has_left)
        def _():
            to_right.wait_recv()

        @pl.when(late)
        def _():
            to_left.wait_recv()

        base = []
        coefs = []
        masks = []
        alive = []
        for where in range(4):
            if where in (0, 3):
                halo = halo_l if where == 0 else halo_r
                there = has_left if where == 0 else has_right
                keep = jnp.full((8, LANES), there.astype(jnp.int32)) > 0
                alive.append(keep)
                base.append([jnp.where(keep, halo[i], 0.0) for i in range(4)])
                rows = [jnp.broadcast_to(halo[4, i : i + 1, :], (8, LANES)) for i in range(6)]
                coefs.append(rows[:4])
                start = tile * sites + (-LANES if where == 0 else sites)
                inside = in_region(start + lane)
                masks.append([jnp.where(inside, rows[4], 0.0), jnp.where(inside, rows[5], 0.0)])
            else:
                c = 0 if where == 1 else chunks - 1
                cut = slice(c * LANES, (c + 1) * LANES)
                alive.append(None)
                base.append([w[i, :, (c + 1) * LANES : (c + 2) * LANES] for i in range(4)])
                coefs.append([coef[i, :, cut] for i in range(4)])
                masks.append([cmask[0, :, cut], cmask[1, :, cut]])
        y = base
        for k in (3, 2, 1, 0):
            out = []
            for where in range(4):
                prev, here, after = y[(where + 3) % 4], y[where], y[(where + 1) % 4]
                lefts = [pltpu.roll(jnp.where(last, p, h), 1, 1) for p, h in zip(prev, here)]
                rights = [
                    pltpu.roll(jnp.where(first, a, h), LANES - 1, 1) for a, h in zip(after, here)
                ]
                new = apply_stage(
                    here,
                    lefts,
                    rights,
                    coefs[where],
                    base[where],
                    STAGE_WEIGHT[k],
                    [par[4 * k + i] for i in range(4)],
                    masks[where],
                )
                if alive[where] is not None:
                    new = [jnp.where(alive[where], x, 0.0) for x in new]
                out.append(new)
            y = out
        for where, c in ((1, 0), (2, chunks - 1)):
            cut = slice(c * LANES, (c + 1) * LANES)
            cs = E4 * coef[4, :, cut]
            sn = E4 * coef[5, :, cut]
            fresh = lane < 4 if where == 1 else lane >= LANES - 4
            for h in range(2):
                up = cs * y[where][2 * h] - sn * y[where][2 * h + 1]
                down = sn * y[where][2 * h] + cs * y[where][2 * h + 1]
                next_out[2 * h, :, cut] = jnp.where(fresh, up, next_out[2 * h, :, cut])
                next_out[2 * h + 1, :, cut] = jnp.where(fresh, down, next_out[2 * h + 1, :, cut])

    @pl.when(jnp.logical_not(early))
    def _():
        redo_ends()

    @pl.when(early)
    def _():
        pl.semaphore_wait(ready, 1)
        to_left_keeper.start()
        to_left.start()

    for q in range(SHARES):
        @pl.when(owner_of(q) != me)
        def _():
            pltpu.make_async_copy(sums.at[q], sums.at[q], ag_recv.at[q]).wait()

        hx, hy, hz = [sums[q, i * run : (i + 1) * run, :] for i in (1, 2, 3)]
        m = [mag_d[i, q * run : (q + 1) * run, :] for i in range(3)]
        turn = time_step * half_d[q * run : (q + 1) * run, :]
        mag_n[0:run, :] = m[0] - turn * (m[1] * hz - m[2] * hy)
        mag_n[run : 2 * run, :] = m[1] - turn * (m[2] * hx - m[0] * hz)
        mag_n[2 * run : 3 * run, :] = m[2] - turn * (m[0] * hy - m[1] * hx)
        for u in range(run):
            cut = slice((q * run + u) * LANES, (q * run + u + 1) * LANES)
            dens_out[:, cut] = sums[q, pl.ds(u, 5, stride=run), :]
            magn_out[:, cut] = mag_n[pl.ds(u, 3, stride=run), :]

    @pl.when(early)
    def _():
        redo_ends()

    @pl.when(has_right)
    def _():
        to_right.wait_send()

    @pl.when(has_left)
    def _():
        to_left.wait_send()
        to_left_keeper.wait_send()

    @pl.when(jnp.logical_not(keeps))
    def _():
        to_keeper.wait_send()

    def settle(q, carry):
        @pl.when(owner_at(q) != me)
        def _():
            pltpu.make_async_copy(part.at[q], part.at[q], rs_send.at[q]).wait()

        @pl.when(owner_at(q) == me)
        def _():
            pltpu.make_async_copy(
                slots.at[q, 0 : nm - 1], slots.at[q, 0 : nm - 1], ag_send.at[q]
            ).wait()

        return carry

    lax.fori_loop(0, SHARES, settle, 0)


def hand_out(next_v, dens_v, magn_v, next_out, dens_out, magn_out, sem):
    copies = [
        pltpu.make_async_copy(src, dst, sem.at[i])
        for i, (src, dst) in enumerate(
            [(next_v, next_out), (dens_v, dens_out), (magn_v, magn_out)]
        )
    ]
    for copy in copies:
        copy.start()
    for copy in copies:
        copy.wait()


def solution(mesh):
    nm = mesh.shape["modes"]
    ns = mesh.shape["sites"]

    def local(
        wave_state,
        potential,
        spin_angle,
        magnet,
        magnetic_mask,
        mode_weight,
        source_amp,
        mode_group,
        energies,
        lead_site,
    ):
        sites = wave_state.shape[2]
        dense = (sites // LANES, LANES)
        modes = wave_state.shape[1]
        rows = 5 * dense[0] // SHARES
        f32 = jnp.float32
        vmem = pltpu.VMEM
        whole = pl.BlockSpec(memory_space=pl.ANY)
        kept = pl.BlockSpec(memory_space=pltpu.VMEM)
        out = pl.pallas_call(
            functools.partial(kernel, nm, ns, sites),
            out_shape=(
                jax.ShapeDtypeStruct(wave_state.shape, f32),
                jax.ShapeDtypeStruct((5, sites), f32),
                jax.ShapeDtypeStruct((3, sites), f32),
            ),
            in_specs=[whole] * 10,
            out_specs=(kept, kept, kept),
            scratch_shapes=[
                vmem(wave_state.shape, f32),
                vmem(dense, f32),
                vmem(dense, f32),
                vmem((3, sites), f32),
                vmem(dense, jnp.int32),
                vmem((1, modes), f32),
                vmem((4, modes), f32),
                vmem((1, modes), jnp.int32),
                vmem((1, energies.shape[0]), f32),
                vmem((1, modes), jnp.int32),
                vmem(dense, f32),
                vmem(dense, f32),
                vmem(dense, f32),
                vmem(dense, f32),
                vmem(dense, f32),
                vmem((3, *dense), f32),
                vmem((3 * rows // 5, LANES), f32),
                vmem((18, modes, LANES), f32),
                vmem((4, modes, sites + 2 * LANES), f32),
                vmem((4, modes, sites + 2 * LANES), f32),
                vmem((4, modes, sites + 2 * LANES), f32),
                vmem((6, modes, sites), f32),
                vmem((2, modes, sites), f32),
                vmem((5, modes, LANES), f32),
                vmem((5, modes, LANES), f32),
                vmem((5, modes, LANES), f32),
                vmem((5, modes, LANES), f32),
                vmem((modes, LANES), f32),
                vmem((modes, LANES), f32),
                vmem((nm, modes, LANES), f32),
                vmem((nm, modes, LANES), f32),
                vmem((SHARES, rows, LANES), f32),
                vmem((SHARES, nm, rows, LANES), f32),
                vmem((SHARES, rows, LANES), f32),
                pltpu.SemaphoreType.DMA((9,)),
                pltpu.SemaphoreType.DMA((SHARES,)),
                pltpu.SemaphoreType.DMA((2,)),
                pltpu.SemaphoreType.DMA((2,)),
                pltpu.SemaphoreType.DMA,
                pltpu.SemaphoreType.DMA,
                pltpu.SemaphoreType.DMA,
                pltpu.SemaphoreType.DMA,
                pltpu.SemaphoreType.DMA((SHARES,)),
                pltpu.SemaphoreType.DMA((SHARES,)),
                pltpu.SemaphoreType.DMA((SHARES,)),
                pltpu.SemaphoreType.DMA((SHARES,)),
                pltpu.SemaphoreType.REGULAR,
            ],
            compiler_params=pltpu.CompilerParams(
                collective_id=0,
                has_side_effects=True,
                vmem_limit_bytes=32 * 1024 * 1024,
            ),
        )(
            *[
                pltpu.with_memory_space_constraint(x, pltpu.HBM)
                for x in (
                    wave_state,
                    potential.reshape(dense),
                    spin_angle.reshape(dense),
                    magnet,
                    magnetic_mask.reshape(dense),
                    mode_weight.reshape(1, modes),
                    source_amp,
                    mode_group.reshape(1, modes),
                    energies.reshape(1, -1),
                    lead_site.reshape(1, modes),
                )
            ]
        )
        return pl.pallas_call(
            hand_out,
            out_shape=tuple(jax.ShapeDtypeStruct(x.shape, f32) for x in out),
            in_specs=[kept] * 3,
            out_specs=(whole,) * 3,
            scratch_shapes=[pltpu.SemaphoreType.DMA((3,))],
            compiler_params=pltpu.CompilerParams(vmem_limit_bytes=2 * 1024 * 1024),
        )(*out)

    return jax.shard_map(
        local,
        mesh=mesh,
        in_specs=(
            P(None, "modes", "sites"),
            P("sites"),
            P("sites"),
            P(None, "sites"),
            P("sites"),
            P("modes"),
            P(None, "modes"),
            P("modes"),
            P(),
            P("modes"),
        ),
        out_specs=(P(None, "modes", "sites"), P(None, "sites"), P(None, "sites")),
        check_vma=False,
    )
```

```python
import functools
import math

import jax
import jax.numpy as jnp
from jax import lax
from jax.experimental import pallas as pl
from jax.experimental.pallas import tpu as pltpu
from jax.sharding import PartitionSpec as P

time_step = 0.6
start_time = 10.0
exchange_coupling = 0.5
MESH = pl.DeviceIdType.MESH
LANES = 128
SHARES = 8
FIRST_TILE_OWNERS = {16: (1, 1, 1, 1, 2, 3, 4, 5), 4: (1, 1, 1, 1, 2, 2, 3, 3)}

E4 = time_step**4 / 24.0
STAGE_WEIGHT = [
    24.0 / time_step**4,
    24.0 / time_step**3,
    12.0 / time_step**2,
    4.0 / time_step,
]


def apply_stage(y, left, right, coef, base, weight, src, masks):
    ur, dr, ui, di = y
    a_up, a_dn, fx, fy = coef
    near = [l + r for l, r in zip(left, right)]
    h_ur = a_up * ur + fx * dr + fy * di - near[0]
    h_dr = a_dn * dr + fx * ur - fy * ui - near[1]
    h_ui = a_up * ui + fx * di - fy * dr - near[2]
    h_di = a_dn * di + fx * ui + fy * ur - near[3]
    cm, sm = masks
    src_ur = cm * src[0] + sm * src[1]
    src_dr = cm * src[1] - sm * src[0]
    src_ui = cm * src[2] + sm * src[3]
    src_di = cm * src[3] - sm * src[2]
    return [
        (weight * base[0] + src_ur) + h_ui,
        (weight * base[1] + src_dr) + h_di,
        (weight * base[2] + src_ui) - h_ur,
        (weight * base[3] + src_di) - h_dr,
    ]


def kernel(
    nm,
    ns,
    sites,
    wave_hbm,
    pot_hbm,
    ang_hbm,
    mag_hbm,
    mask_hbm,
    wt_hbm,
    amp_hbm,
    grp_hbm,
    en_hbm,
    lead_hbm,
    next_out,
    dens_out,
    magn_out,
    wave,
    pot,
    ang,
    mag,
    mask,
    wt,
    amp,
    grp,
    en,
    lead,
    cos_d,
    sin_d,
    cos2_d,
    sin2_d,
    half_d,
    mag_d,
    mag_n,
    par,
    w,
    ya,
    yb,
    coef,
    cmask,
    edge_l,
    edge_r,
    halo_l,
    halo_r,
    bond_a,
    bond_b,
    slots_a,
    slots_b,
    part,
    slots,
    sums,
    in_sem,
    wave_sem,
    halo_send,
    halo_recv,
    a_send,
    a_recv,
    b_send,
    b_recv,
    rs_send,
    rs_recv,
    ag_send,
    ag_recv,
    ready,
):
    chunks = sites // LANES
    run = chunks // SHARES
    unroll = 4
    me = lax.axis_index("modes")
    tile = lax.axis_index("sites")
    turn_tile = ns // 2
    has_left = tile > 0
    has_right = tile < ns - 1
    at_turn = tile == turn_tile
    before_turn = tile == turn_tile - 1
    early = at_turn | ((tile == 1) & (me == 0))
    late = before_turn | ((tile == 0) & (me == 0))
    usual = [q * min(nm, SHARES) // SHARES for q in range(SHARES)]
    special = FIRST_TILE_OWNERS.get(nm, usual)

    def owner_of(q):
        return jnp.where(tile == 0, jnp.int32(special[q]), jnp.int32(usual[q]))

    def owner_at(q):
        found = owner_of(0)
        for i in range(1, SHARES):
            found = jnp.where(q == i, owner_of(i), found)
        return found

    def among(devices):
        found = me == devices[0]
        for d in devices[1:]:
            found = found | (me == d)
        return found

    is_owner = jnp.where(tile == 0, among(sorted(set(special))).astype(jnp.int32), among(sorted(set(usual))).astype(jnp.int32))
    owner_count = jnp.where(tile == 0, len(set(special)), len(set(usual)))
    keeper = owner_of(SHARES - 1)
    keeps = me == keeper
    left_keeper = jnp.where(tile == 1, jnp.int32(special[-1]), jnp.int32(usual[-1]))
    order = [j for j in (1, 3, 0, 2, 5, 7, 4, 6, 13, 15, 12, 14, 9, 11, 8, 10) if j < nm]

    def signal(sem, where):
        pl.semaphore_signal(sem, inc=1, device_id=where, device_id_type=MESH)

    def send(src, dst, send_sem, recv_sem, where):
        return pltpu.make_async_remote_copy(
            src_ref=src,
            dst_ref=dst,
            send_sem=send_sem,
            recv_sem=recv_sem,
            device_id=where,
            device_id_type=MESH,
        )

    barrier = pltpu.get_barrier_semaphore()

    @pl.when(is_owner == 1)
    def _():
        for k in range(1, nm):
            signal(barrier, {"modes": me ^ k})

    @pl.when(has_right & jnp.logical_not(late))
    def _():
        signal(barrier, {"sites": tile + 1})

    @pl.when(early)
    def _():
        signal(barrier, {"sites": tile - 1})

    @pl.when(keeps & has_right & jnp.logical_not(before_turn))
    def _():
        for m in range(nm):
            signal(barrier, {"modes": jnp.int32(m), "sites": tile + 1})

    fetches = [
        pltpu.make_async_copy(src, dst, in_sem.at[i])
        for i, (src, dst) in enumerate(
            [
                (wt_hbm, wt),
                (amp_hbm, amp),
                (grp_hbm, grp),
                (en_hbm, en),
                (lead_hbm, lead),
                (ang_hbm, ang),
                (pot_hbm, pot),
                (mag_hbm, mag),
                (mask_hbm, mask),
            ]
        )
    ]

    def piece(q):
        cut = pl.ds(pl.multiple_of(q * (run * LANES), LANES), run * LANES)
        return pltpu.make_async_copy(
            wave_hbm.at[:, :, cut], wave.at[:, :, cut], wave_sem.at[q]
        )

    for fetch in fetches:
        fetch.start()
    for q in (0, SHARES - 1, *range(1, SHARES - 1)):
        piece(q).start()
    pl.semaphore_wait(
        barrier,
        owner_count
        - is_owner
        + (has_left & jnp.logical_not(early)).astype(jnp.int32)
        + (has_left & jnp.logical_not(at_turn)).astype(jnp.int32)
        + late.astype(jnp.int32),
    )

    @pl.when(late)
    def _():
        signal(ready, {"sites": tile + 1})

    for fetch in fetches[:5]:
        fetch.wait()

    group = grp[...]
    energy_row = en[...]
    energy = jnp.zeros(group.shape, jnp.float32)
    for g in range(energy_row.shape[1]):
        energy = energy + jnp.where(group == g, energy_row[:, g : g + 1], 0.0)
    amp_re = amp[0:2, :]
    amp_im = amp[2:4, :]
    rate = []
    for offset in (0.0, 0.5 * time_step, time_step):
        phase = energy * (start_time + offset)
        cosine = jnp.cos(phase)
        sine = jnp.sin(phase)
        rate.append(
            (
                amp_im * cosine - amp_re * sine,
                -(amp_re * cosine + amp_im * sine),
            )
        )
    mixes = [
        [time_step / 6.0, 4.0 * time_step / 6.0, time_step / 6.0],
        [time_step / 6.0, 2.0 * time_step / 6.0, 0.0],
        [time_step / 6.0, time_step / 6.0, 0.0],
        [time_step / 4.0, 0.0, 0.0],
    ]
    modes = group.shape[1]
    diag = lax.broadcasted_iota(jnp.int32, (modes, modes), 0) == lax.broadcasted_iota(
        jnp.int32, (modes, modes), 1
    )

    def column(row):
        spread = jnp.where(diag, jnp.broadcast_to(row, (modes, modes)), 0.0)
        return jnp.broadcast_to(jnp.sum(spread, axis=1, keepdims=True), (modes, LANES))

    for k in range(4):
        for half in range(2):
            mixed = sum(
                (STAGE_WEIGHT[k] * mixes[k][t]) * rate[t][half]
                for t in range(3)
                if mixes[k][t] != 0.0
            )
            for spin in range(2):
                par[4 * k + 2 * half + spin] = column(mixed[spin : spin + 1, :])
    par[16] = column(wt[...])
    par[17] = column(lead[...].astype(jnp.float32))

    for fetch in fetches[5:9]:
        fetch.wait()
    angle = ang[...]
    cosine = jnp.cos(angle)
    sine = jnp.sin(angle)
    cos_d[...] = cosine
    sin_d[...] = sine
    cos2_d[...] = 1.0 - 2.0 * sine * sine
    sin2_d[...] = 2.0 * sine * cosine
    half_d[...] = exchange_coupling * mask[...].astype(jnp.float32)

    zero = jnp.zeros((8, LANES), jnp.float32)
    for buf in (w, ya, yb):
        for c in range(4):
            buf[c, :, 0:LANES] = zero
            buf[c, :, LANES + sites : 2 * LANES + sites] = zero
    lane = lax.broadcasted_iota(jnp.int32, (8, LANES), 1)
    sub = lax.broadcasted_iota(jnp.int32, (8, LANES), 0)
    first = lane == 0
    last = lane == LANES - 1
    span = float(sites * ns // 8)

    def in_region(position):
        away = position.astype(jnp.float32) - par[17]
        return (away >= 0.0) & (away < span)

    def row(ref, i):
        return jnp.broadcast_to(ref[pl.ds(i, 1), :], (8, LANES))

    def at(c, shift=0):
        return pl.ds(pl.multiple_of(c * LANES, LANES) + shift * LANES, LANES)

    def site_terms(c):
        cs = row(cos_d, c)
        sn = row(sin_d, c)
        c2 = row(cos2_d, c)
        s2 = row(sin2_d, c)
        half = row(half_d, c)
        field = [half * jnp.broadcast_to(mag[i : i + 1, at(c)], (8, LANES)) for i in range(3)]
        v = row(pot, c)
        fz = c2 * field[2] + s2 * field[0]
        coef[0, :, at(c)] = v + fz
        coef[1, :, at(c)] = v - fz
        coef[2, :, at(c)] = c2 * field[0] - s2 * field[2]
        coef[3, :, at(c)] = field[1]
        coef[4, :, at(c)] = cs
        coef[5, :, at(c)] = sn
        inside = in_region(tile * sites + c * LANES + lane)
        cmask[0, :, at(c)] = jnp.where(inside, cs, 0.0)
        cmask[1, :, at(c)] = jnp.where(inside, sn, 0.0)

    def rotate(q):
        piece(q).wait()
        for u in range(run):
            c = q * run + u
            cs = row(cos_d, c)
            sn = row(sin_d, c)
            for part_i in range(2):
                up = wave[2 * part_i, :, at(c)]
                down = wave[2 * part_i + 1, :, at(c)]
                w[2 * part_i, :, at(c, 1)] = cs * up + sn * down
                w[2 * part_i + 1, :, at(c, 1)] = cs * down - sn * up

    site_terms(0)
    site_terms(chunks - 1)
    rotate(0)
    rotate(SHARES - 1)

    all_modes = float(modes * nm)
    root = 1.0 / math.sqrt(all_modes)
    weight = root * par[16]

    for edge, c in ((edge_l, 0), (edge_r, chunks - 1)):
        for i in range(4):
            edge[i] = w[i, :, (c + 1) * LANES : (c + 2) * LANES]
        rows = zero
        for i in range(6):
            rows = jnp.where(sub == i, coef[i, :, c * LANES : (c + 1) * LANES], rows)
        edge[4] = rows
    left_factor = zero
    right_factor = zero
    for i in range(4):
        left_factor = jnp.where(lane == i, pltpu.roll(edge_r[i], 1 + i, 1), left_factor)
        other = edge_l[(i + 2) % 4]
        other = pltpu.roll(other, i, 1) if i else other
        right_factor = jnp.where(lane == i, other if i < 2 else -other, right_factor)
    bond_a[...] = 2.0 * (weight * left_factor)
    bond_b[...] = right_factor

    to_left = send(
        edge_l, halo_r, halo_send.at[0], halo_recv.at[0], {"sites": jnp.maximum(tile - 1, 0)}
    )
    to_right = send(
        edge_r, halo_l, halo_send.at[1], halo_recv.at[1], {"sites": jnp.minimum(tile + 1, ns - 1)}
    )
    to_keeper = send(bond_a, slots_a.at[me], a_send, a_recv, {"modes": keeper})
    to_left_keeper = send(
        bond_b,
        slots_b.at[me],
        b_send,
        b_recv,
        {"modes": left_keeper, "sites": jnp.maximum(tile - 1, 0)},
    )

    @pl.when(late)
    def _():
        to_right.start()

    @pl.when(has_left & jnp.logical_not(at_turn))
    def _():
        to_left_keeper.start()

    @pl.when(has_left & jnp.logical_not(early))
    def _():
        to_left.start()

    @pl.when(jnp.logical_not(keeps))
    def _():
        to_keeper.start()

    def current(wc, wn, weight):
        after = [jnp.where(first, n, c) for c, n in zip(wc, wn)]
        after = [pltpu.roll(a, LANES - 1, 1) for a in after]
        return weight * (
            wc[0] * after[2] - wc[2] * after[0] + (wc[1] * after[3] - wc[3] * after[1])
        )

    def down_sum(x):
        return jnp.sum(x, axis=0, keepdims=True)

    odd = (sub & 1) == 1
    upper_pair = (sub & 2) == 2
    lower_half = sub < 4

    def fold(x, y, other, shift):
        return jnp.where(other, y, x) + pltpu.roll(jnp.where(other, x, y), 8 - shift, 0)

    def fold_four(x):
        return fold(fold(x[0], x[1], odd, 1), fold(x[2], x[3], odd, 1), upper_pair, 2)

    def fold_eight(x):
        return fold(fold_four(x[:4]), fold_four(x[4:]), jnp.logical_not(lower_half), 4)

    first_scale = jnp.where(lower_half, root, 2.0)
    second_scale = jnp.where(lower_half, 2.0, 1.0)

    def density(q):
        wc = [w[i, :, at(q * run, 1)] for i in range(4)]
        tiles = [[], [], [], [], []]
        for u in range(run):
            c = q * run + u
            wn = [w[i, :, at(c, 2)] for i in range(4)]
            ur, dr, ui, di = [wave[i, :, at(c)] for i in range(4)]
            wur, wdr, wui, wdi = [weight * x for x in (ur, dr, ui, di)]
            up = wur * ur + wui * ui
            dn = wdr * dr + wdi * di
            tiles[0].append(up + dn)
            tiles[1].append(wur * dr + wui * di)
            tiles[2].append(wur * di - wui * dr)
            tiles[3].append(up - dn)
            tiles[4].append(current(wc, wn, weight))
            wc = wn
        part[q, 0:8, :] = first_scale * fold_eight(tiles[0] + tiles[1])
        part[q, 8:16, :] = second_scale * fold_eight(tiles[2] + tiles[3])
        bonds = fold_four(tiles[4])
        part[q, 16:20, :] = (2.0 * (bonds + pltpu.roll(bonds, 4, 0)))[0:4, :]
        owner = owner_at(q)

        @pl.when(owner != me)
        def _():
            send(part.at[q], slots.at[q, me], rs_send.at[q], rs_recv.at[q], {"modes": owner}).start()

    def stream(q, carry):
        rotate(q)
        density(q - 1)
        return carry

    def finish(q, carry):
        density(q)
        return carry

    lax.fori_loop(1, SHARES - 1, stream, 0)
    lax.fori_loop(SHARES - 2, SHARES, finish, 0)

    def stage_pass(src_ref, dst_ref, k):
        def body(block, carry):
            def load(c, shift):
                return [src_ref[i, :, at(c, shift)] for i in range(4)]

            c0 = block * unroll
            prev = load(c0, 0)
            here = load(c0, 1)
            for u in range(unroll):
                c = c0 + u
                after = load(c, 2)
                lefts = [pltpu.roll(jnp.where(last, p, h), 1, 1) for p, h in zip(prev, here)]
                rights = [
                    pltpu.roll(jnp.where(first, a, h), LANES - 1, 1) for a, h in zip(after, here)
                ]
                base = here if k == 3 else [w[i, :, at(c, 1)] for i in range(4)]
                out = apply_stage(
                    here,
                    lefts,
                    rights,
                    [coef[i, :, at(c)] for i in range(4)],
                    base,
                    STAGE_WEIGHT[k],
                    [par[4 * k + i] for i in range(4)],
                    [cmask[0, :, at(c)], cmask[1, :, at(c)]],
                )
                if k > 0:
                    for i in range(4):
                        dst_ref[i, :, at(c, 1)] = out[i]
                else:
                    cs = E4 * coef[4, :, at(c)]
                    sn = E4 * coef[5, :, at(c)]
                    for h in range(2):
                        next_out[2 * h, :, at(c)] = cs * out[2 * h] - sn * out[2 * h + 1]
                        next_out[2 * h + 1, :, at(c)] = sn * out[2 * h] + cs * out[2 * h + 1]
                prev, here = here, after
            return carry

        lax.fori_loop(0, chunks // unroll, body, 0)

    def terms(block, carry):
        for u in range(unroll):
            site_terms(block * unroll + u)
        return carry

    lax.fori_loop(0, chunks // unroll, terms, 0)
    stage_pass(w, ya, 3)
    stage_pass(ya, yb, 2)
    stage_pass(yb, ya, 1)

    @pl.when(has_right & jnp.logical_not(late))
    def _():
        to_left.wait_recv()
        to_right.start()

    def add_up(q, carry):
        owns = owner_at(q) == me

        @pl.when(owns)
        def _():
            slots[q, me] = part[q]
            pltpu.make_async_copy(
                slots.at[q, 0 : nm - 1], slots.at[q, 0 : nm - 1], rs_recv.at[q]
            ).wait()
            total = slots[q, 0]
            for d in range(1, nm):
                total = total + slots[q, d]
            sums[q] = total

            @pl.when(q == SHARES - 1)
            def _():
                pltpu.make_async_copy(
                    slots_a.at[0 : nm - 1], slots_a.at[0 : nm - 1], a_recv
                ).wait()

            @pl.when((q == SHARES - 1) & has_right)
            def _():
                pltpu.make_async_copy(slots_b, slots_b, b_recv).wait()
                bond = bond_a[...] * slots_b[me]
                for k in range(1, nm):
                    bond = bond + slots_a[me ^ k] * slots_b[me ^ k]
                bond = jnp.sum(down_sum(bond), axis=1, keepdims=True)
                end = 5 * run - 1
                sums[q, end : end + 1, :] = sums[q, end : end + 1, :] + jnp.where(
                    last[0:1], jnp.broadcast_to(bond, (1, LANES)), 0.0
                )

            for j in order:
                @pl.when(me != j)
                def _():
                    send(
                        sums.at[q],
                        sums.at[q],
                        ag_send.at[q],
                        ag_recv.at[q],
                        {"modes": jnp.int32(j)},
                    ).start()

        return carry

    lax.fori_loop(0, SHARES, add_up, 0)

    stage_pass(ya, None, 0)
    for i in range(3):
        for c in range(chunks):
            mag_d[i, c : c + 1, :] = mag[i : i + 1, c * LANES : (c + 1) * LANES]

    def redo_ends():
        @pl.when(has_left)
        def _():
            to_right.wait_recv()

        @pl.when(late)
        def _():
            to_left.wait_recv()

        base = []
        coefs = []
        masks = []
        alive = []
        for where in range(4):
            if where in (0, 3):
                halo = halo_l if where == 0 else halo_r
                there = has_left if where == 0 else has_right
                keep = jnp.full((8, LANES), there.astype(jnp.int32)) > 0
                alive.append(keep)
                base.append([jnp.where(keep, halo[i], 0.0) for i in range(4)])
                rows = [jnp.broadcast_to(halo[4, i : i + 1, :], (8, LANES)) for i in range(6)]
                coefs.append(rows[:4])
                start = tile * sites + (-LANES if where == 0 else sites)
                inside = in_region(start + lane)
                masks.append([jnp.where(inside, rows[4], 0.0), jnp.where(inside, rows[5], 0.0)])
            else:
                c = 0 if where == 1 else chunks - 1
                cut = slice(c * LANES, (c + 1) * LANES)
                alive.append(None)
                base.append([w[i, :, (c + 1) * LANES : (c + 2) * LANES] for i in range(4)])
                coefs.append([coef[i, :, cut] for i in range(4)])
                masks.append([cmask[0, :, cut], cmask[1, :, cut]])
        y = base
        for k in (3, 2, 1, 0):
            out = []
            for where in range(4):
                prev, here, after = y[(where + 3) % 4], y[where], y[(where + 1) % 4]
                lefts = [pltpu.roll(jnp.where(last, p, h), 1, 1) for p, h in zip(prev, here)]
                rights = [
                    pltpu.roll(jnp.where(first, a, h), LANES - 1, 1) for a, h in zip(after, here)
                ]
                new = apply_stage(
                    here,
                    lefts,
                    rights,
                    coefs[where],
                    base[where],
                    STAGE_WEIGHT[k],
                    [par[4 * k + i] for i in range(4)],
                    masks[where],
                )
                if alive[where] is not None:
                    new = [jnp.where(alive[where], x, 0.0) for x in new]
                out.append(new)
            y = out
        for where, c in ((1, 0), (2, chunks - 1)):
            cut = slice(c * LANES, (c + 1) * LANES)
            cs = E4 * coef[4, :, cut]
            sn = E4 * coef[5, :, cut]
            fresh = lane < 4 if where == 1 else lane >= LANES - 4
            for h in range(2):
                up = cs * y[where][2 * h] - sn * y[where][2 * h + 1]
                down = sn * y[where][2 * h] + cs * y[where][2 * h + 1]
                next_out[2 * h, :, cut] = jnp.where(fresh, up, next_out[2 * h, :, cut])
                next_out[2 * h + 1, :, cut] = jnp.where(fresh, down, next_out[2 * h + 1, :, cut])

    @pl.when(jnp.logical_not(early))
    def _():
        redo_ends()

    @pl.when(early)
    def _():
        pl.semaphore_wait(ready, 1)
        to_left.start()

    @pl.when(at_turn)
    def _():
        to_left_keeper.start()

    for q in range(SHARES):
        @pl.when(owner_of(q) != me)
        def _():
            pltpu.make_async_copy(sums.at[q], sums.at[q], ag_recv.at[q]).wait()

        hx, hy, hz = [sums[q, i * run : (i + 1) * run, :] for i in (1, 2, 3)]
        m = [mag_d[i, q * run : (q + 1) * run, :] for i in range(3)]
        turn = time_step * half_d[q * run : (q + 1) * run, :]
        mag_n[0:run, :] = m[0] - turn * (m[1] * hz - m[2] * hy)
        mag_n[run : 2 * run, :] = m[1] - turn * (m[2] * hx - m[0] * hz)
        mag_n[2 * run : 3 * run, :] = m[2] - turn * (m[0] * hy - m[1] * hx)
        for u in range(run):
            cut = slice((q * run + u) * LANES, (q * run + u + 1) * LANES)
            dens_out[:, cut] = sums[q, pl.ds(u, 5, stride=run), :]
            magn_out[:, cut] = mag_n[pl.ds(u, 3, stride=run), :]

    @pl.when(early)
    def _():
        redo_ends()

    @pl.when(has_right)
    def _():
        to_right.wait_send()

    @pl.when(has_left)
    def _():
        to_left.wait_send()
        to_left_keeper.wait_send()

    @pl.when(jnp.logical_not(keeps))
    def _():
        to_keeper.wait_send()

    def settle(q, carry):
        @pl.when(owner_at(q) != me)
        def _():
            pltpu.make_async_copy(part.at[q], part.at[q], rs_send.at[q]).wait()

        @pl.when(owner_at(q) == me)
        def _():
            pltpu.make_async_copy(
                slots.at[q, 0 : nm - 1], slots.at[q, 0 : nm - 1], ag_send.at[q]
            ).wait()

        return carry

    lax.fori_loop(0, SHARES, settle, 0)


def hand_out(next_v, dens_v, magn_v, next_out, dens_out, magn_out, sem):
    copies = [
        pltpu.make_async_copy(src, dst, sem.at[i])
        for i, (src, dst) in enumerate(
            [(next_v, next_out), (dens_v, dens_out), (magn_v, magn_out)]
        )
    ]
    for copy in copies:
        copy.start()
    for copy in copies:
        copy.wait()


def solution(mesh):
    nm = mesh.shape["modes"]
    ns = mesh.shape["sites"]

    def local(
        wave_state,
        potential,
        spin_angle,
        magnet,
        magnetic_mask,
        mode_weight,
        source_amp,
        mode_group,
        energies,
        lead_site,
    ):
        sites = wave_state.shape[2]
        dense = (sites // LANES, LANES)
        modes = wave_state.shape[1]
        rows = 5 * dense[0] // SHARES
        f32 = jnp.float32
        vmem = pltpu.VMEM
        whole = pl.BlockSpec(memory_space=pl.ANY)
        kept = pl.BlockSpec(memory_space=pltpu.VMEM)
        out = pl.pallas_call(
            functools.partial(kernel, nm, ns, sites),
            out_shape=(
                jax.ShapeDtypeStruct(wave_state.shape, f32),
                jax.ShapeDtypeStruct((5, sites), f32),
                jax.ShapeDtypeStruct((3, sites), f32),
            ),
            in_specs=[whole] * 10,
            out_specs=(kept, kept, kept),
            scratch_shapes=[
                vmem(wave_state.shape, f32),
                vmem(dense, f32),
                vmem(dense, f32),
                vmem((3, sites), f32),
                vmem(dense, jnp.int32),
                vmem((1, modes), f32),
                vmem((4, modes), f32),
                vmem((1, modes), jnp.int32),
                vmem((1, energies.shape[0]), f32),
                vmem((1, modes), jnp.int32),
                vmem(dense, f32),
                vmem(dense, f32),
                vmem(dense, f32),
                vmem(dense, f32),
                vmem(dense, f32),
                vmem((3, *dense), f32),
                vmem((3 * rows // 5, LANES), f32),
                vmem((18, modes, LANES), f32),
                vmem((4, modes, sites + 2 * LANES), f32),
                vmem((4, modes, sites + 2 * LANES), f32),
                vmem((4, modes, sites + 2 * LANES), f32),
                vmem((6, modes, sites), f32),
                vmem((2, modes, sites), f32),
                vmem((5, modes, LANES), f32),
                vmem((5, modes, LANES), f32),
                vmem((5, modes, LANES), f32),
                vmem((5, modes, LANES), f32),
                vmem((modes, LANES), f32),
                vmem((modes, LANES), f32),
                vmem((nm, modes, LANES), f32),
                vmem((nm, modes, LANES), f32),
                vmem((SHARES, rows, LANES), f32),
                vmem((SHARES, nm, rows, LANES), f32),
                vmem((SHARES, rows, LANES), f32),
                pltpu.SemaphoreType.DMA((9,)),
                pltpu.SemaphoreType.DMA((SHARES,)),
                pltpu.SemaphoreType.DMA((2,)),
                pltpu.SemaphoreType.DMA((2,)),
                pltpu.SemaphoreType.DMA,
                pltpu.SemaphoreType.DMA,
                pltpu.SemaphoreType.DMA,
                pltpu.SemaphoreType.DMA,
                pltpu.SemaphoreType.DMA((SHARES,)),
                pltpu.SemaphoreType.DMA((SHARES,)),
                pltpu.SemaphoreType.DMA((SHARES,)),
                pltpu.SemaphoreType.DMA((SHARES,)),
                pltpu.SemaphoreType.REGULAR,
            ],
            compiler_params=pltpu.CompilerParams(
                collective_id=0,
                has_side_effects=True,
                vmem_limit_bytes=32 * 1024 * 1024,
            ),
        )(
            *[
                pltpu.with_memory_space_constraint(x, pltpu.HBM)
                for x in (
                    wave_state,
                    potential.reshape(dense),
                    spin_angle.reshape(dense),
                    magnet,
                    magnetic_mask.reshape(dense),
                    mode_weight.reshape(1, modes),
                    source_amp,
                    mode_group.reshape(1, modes),
                    energies.reshape(1, -1),
                    lead_site.reshape(1, modes),
                )
            ]
        )
        return pl.pallas_call(
            hand_out,
            out_shape=tuple(jax.ShapeDtypeStruct(x.shape, f32) for x in out),
            in_specs=[kept] * 3,
            out_specs=(whole,) * 3,
            scratch_shapes=[pltpu.SemaphoreType.DMA((3,))],
            compiler_params=pltpu.CompilerParams(vmem_limit_bytes=2 * 1024 * 1024),
        )(*out)

    return jax.shard_map(
        local,
        mesh=mesh,
        in_specs=(
            P(None, "modes", "sites"),
            P("sites"),
            P("sites"),
            P(None, "sites"),
            P("sites"),
            P("modes"),
            P(None, "modes"),
            P("modes"),
            P(),
            P("modes"),
        ),
        out_specs=(P(None, "modes", "sites"), P(None, "sites"), P(None, "sites")),
        check_vma=False,
    )
```

```python
import functools
import math

import jax
import jax.numpy as jnp
from jax import lax
from jax.experimental import pallas as pl
from jax.experimental.pallas import tpu as pltpu
from jax.sharding import PartitionSpec as P

time_step = 0.6
start_time = 10.0
exchange_coupling = 0.5
MESH = pl.DeviceIdType.MESH
LANES = 128
SHARES = 8
FIRST_TILE_OWNERS = {16: (1, 1, 1, 1, 2, 3, 4, 5), 4: (1, 1, 1, 1, 2, 2, 3, 3)}

E4 = time_step**4 / 24.0
STAGE_WEIGHT = [
    24.0 / time_step**4,
    24.0 / time_step**3,
    12.0 / time_step**2,
    4.0 / time_step,
]


def apply_stage(y, left, right, coef, base, weight, src, masks):
    ur, dr, ui, di = y
    a_up, a_dn, fx, fy = coef
    near = [l + r for l, r in zip(left, right)]
    h_ur = a_up * ur + fx * dr + fy * di - near[0]
    h_dr = a_dn * dr + fx * ur - fy * ui - near[1]
    h_ui = a_up * ui + fx * di - fy * dr - near[2]
    h_di = a_dn * di + fx * ui + fy * ur - near[3]
    cm, sm = masks
    src_ur = cm * src[0] + sm * src[1]
    src_dr = cm * src[1] - sm * src[0]
    src_ui = cm * src[2] + sm * src[3]
    src_di = cm * src[3] - sm * src[2]
    return [
        (weight * base[0] + src_ur) + h_ui,
        (weight * base[1] + src_dr) + h_di,
        (weight * base[2] + src_ui) - h_ur,
        (weight * base[3] + src_di) - h_dr,
    ]


def kernel(
    nm,
    ns,
    sites,
    wave_hbm,
    pot_hbm,
    ang_hbm,
    mag_hbm,
    mask_hbm,
    wt_hbm,
    amp_hbm,
    grp_hbm,
    en_hbm,
    lead_hbm,
    next_out,
    dens_out,
    magn_out,
    wave,
    pot,
    ang,
    mag,
    mask,
    wt,
    amp,
    grp,
    en,
    lead,
    cos_d,
    sin_d,
    cos2_d,
    sin2_d,
    half_d,
    mag_d,
    mag_n,
    par,
    w,
    ya,
    yb,
    coef,
    cmask,
    edge_l,
    edge_r,
    halo_l,
    halo_r,
    bond_a,
    bond_b,
    slots_a,
    slots_b,
    part,
    slots,
    sums,
    in_sem,
    wave_sem,
    halo_send,
    halo_recv,
    a_send,
    a_recv,
    b_send,
    b_recv,
    rs_send,
    rs_recv,
    ag_send,
    ag_recv,
    ready,
):
    chunks = sites // LANES
    run = chunks // SHARES
    unroll = 4
    me = lax.axis_index("modes")
    tile = lax.axis_index("sites")
    turn_tile = ns // 2
    has_left = tile > 0
    has_right = tile < ns - 1
    at_turn = tile == turn_tile
    before_turn = tile == turn_tile - 1
    early = at_turn | before_turn | ((tile == 1) & (me == 0))
    late = before_turn | (tile == turn_tile - 2) | ((tile == 0) & (me == 0))
    usual = [q * min(nm, SHARES) // SHARES for q in range(SHARES)]
    usual = [1, 3, 5, 7, 1, 3, 5, 7] if nm == 16 else usual
    special = FIRST_TILE_OWNERS.get(nm, usual)

    def owner_of(q):
        return jnp.where(tile == 0, jnp.int32(special[q]), jnp.int32(usual[q]))

    def owner_at(q):
        found = owner_of(0)
        for i in range(1, SHARES):
            found = jnp.where(q == i, owner_of(i), found)
        return found

    def among(devices):
        found = me == devices[0]
        for d in devices[1:]:
            found = found | (me == d)
        return found

    is_owner = jnp.where(tile == 0, among(sorted(set(special))).astype(jnp.int32), among(sorted(set(usual))).astype(jnp.int32))
    owner_count = jnp.where(tile == 0, len(set(special)), len(set(usual)))
    keeper = owner_of(SHARES - 1)
    keeps = me == keeper
    left_keeper = jnp.where(tile == 1, jnp.int32(special[-1]), jnp.int32(usual[-1]))
    order = [j for j in (1, 3, 0, 2, 5, 7, 4, 6, 13, 15, 12, 14, 9, 11, 8, 10) if j < nm]

    def signal(sem, where):
        pl.semaphore_signal(sem, inc=1, device_id=where, device_id_type=MESH)

    def send(src, dst, send_sem, recv_sem, where):
        return pltpu.make_async_remote_copy(
            src_ref=src,
            dst_ref=dst,
            send_sem=send_sem,
            recv_sem=recv_sem,
            device_id=where,
            device_id_type=MESH,
        )

    barrier = pltpu.get_barrier_semaphore()

    @pl.when(is_owner == 1)
    def _():
        for k in range(1, nm):
            signal(barrier, {"modes": me ^ k})

    @pl.when(has_right & jnp.logical_not(late))
    def _():
        signal(barrier, {"sites": tile + 1})

    @pl.when(early)
    def _():
        signal(barrier, {"sites": tile - 1})

    @pl.when(keeps & has_right & (tile != turn_tile - 2) & jnp.logical_not(before_turn))
    def _():
        for m in range(nm):
            signal(barrier, {"modes": jnp.int32(m), "sites": tile + 1})

    fetches = [
        pltpu.make_async_copy(src, dst, in_sem.at[i])
        for i, (src, dst) in enumerate(
            [
                (wt_hbm, wt),
                (amp_hbm, amp),
                (grp_hbm, grp),
                (en_hbm, en),
                (lead_hbm, lead),
                (ang_hbm, ang),
                (pot_hbm, pot),
                (mag_hbm, mag),
                (mask_hbm, mask),
            ]
        )
    ]

    def piece(q):
        cut = pl.ds(pl.multiple_of(q * (run * LANES), LANES), run * LANES)
        return pltpu.make_async_copy(
            wave_hbm.at[:, :, cut], wave.at[:, :, cut], wave_sem.at[q]
        )

    for fetch in fetches:
        fetch.start()
    for q in (0, SHARES - 1, *range(1, SHARES - 1)):
        piece(q).start()
    pl.semaphore_wait(
        barrier,
        owner_count
        - is_owner
        + (has_left & jnp.logical_not(early)).astype(jnp.int32)
        + (has_left & jnp.logical_not(at_turn | before_turn)).astype(jnp.int32)
        + late.astype(jnp.int32),
    )

    @pl.when(late)
    def _():
        signal(ready, {"sites": tile + 1})

    for fetch in fetches[:5]:
        fetch.wait()

    group = grp[...]
    energy_row = en[...]
    energy = jnp.zeros(group.shape, jnp.float32)
    for g in range(energy_row.shape[1]):
        energy = energy + jnp.where(group == g, energy_row[:, g : g + 1], 0.0)
    amp_re = amp[0:2, :]
    amp_im = amp[2:4, :]
    rate = []
    for offset in (0.0, 0.5 * time_step, time_step):
        phase = energy * (start_time + offset)
        cosine = jnp.cos(phase)
        sine = jnp.sin(phase)
        rate.append(
            (
                amp_im * cosine - amp_re * sine,
                -(amp_re * cosine + amp_im * sine),
            )
        )
    mixes = [
        [time_step / 6.0, 4.0 * time_step / 6.0, time_step / 6.0],
        [time_step / 6.0, 2.0 * time_step / 6.0, 0.0],
        [time_step / 6.0, time_step / 6.0, 0.0],
        [time_step / 4.0, 0.0, 0.0],
    ]
    modes = group.shape[1]
    diag = lax.broadcasted_iota(jnp.int32, (modes, modes), 0) == lax.broadcasted_iota(
        jnp.int32, (modes, modes), 1
    )

    def column(row):
        spread = jnp.where(diag, jnp.broadcast_to(row, (modes, modes)), 0.0)
        return jnp.broadcast_to(jnp.sum(spread, axis=1, keepdims=True), (modes, LANES))

    for k in range(4):
        for half in range(2):
            mixed = sum(
                (STAGE_WEIGHT[k] * mixes[k][t]) * rate[t][half]
                for t in range(3)
                if mixes[k][t] != 0.0
            )
            for spin in range(2):
                par[4 * k + 2 * half + spin] = column(mixed[spin : spin + 1, :])
    par[16] = column(wt[...])
    par[17] = column(lead[...].astype(jnp.float32))

    for fetch in fetches[5:9]:
        fetch.wait()
    angle = ang[...]
    cosine = jnp.cos(angle)
    sine = jnp.sin(angle)
    cos_d[...] = cosine
    sin_d[...] = sine
    cos2_d[...] = 1.0 - 2.0 * sine * sine
    sin2_d[...] = 2.0 * sine * cosine
    half_d[...] = exchange_coupling * mask[...].astype(jnp.float32)

    zero = jnp.zeros((8, LANES), jnp.float32)
    for buf in (w, ya, yb):
        for c in range(4):
            buf[c, :, 0:LANES] = zero
            buf[c, :, LANES + sites : 2 * LANES + sites] = zero
    lane = lax.broadcasted_iota(jnp.int32, (8, LANES), 1)
    sub = lax.broadcasted_iota(jnp.int32, (8, LANES), 0)
    first = lane == 0
    last = lane == LANES - 1
    span = float(sites * ns // 8)

    def in_region(position):
        away = position.astype(jnp.float32) - par[17]
        return (away >= 0.0) & (away < span)

    def row(ref, i):
        return jnp.broadcast_to(ref[pl.ds(i, 1), :], (8, LANES))

    def at(c, shift=0):
        return pl.ds(pl.multiple_of(c * LANES, LANES) + shift * LANES, LANES)

    def site_terms(c):
        cs = row(cos_d, c)
        sn = row(sin_d, c)
        c2 = row(cos2_d, c)
        s2 = row(sin2_d, c)
        half = row(half_d, c)
        field = [half * jnp.broadcast_to(mag[i : i + 1, at(c)], (8, LANES)) for i in range(3)]
        v = row(pot, c)
        fz = c2 * field[2] + s2 * field[0]
        coef[0, :, at(c)] = v + fz
        coef[1, :, at(c)] = v - fz
        coef[2, :, at(c)] = c2 * field[0] - s2 * field[2]
        coef[3, :, at(c)] = field[1]
        coef[4, :, at(c)] = cs
        coef[5, :, at(c)] = sn
        inside = in_region(tile * sites + c * LANES + lane)
        cmask[0, :, at(c)] = jnp.where(inside, cs, 0.0)
        cmask[1, :, at(c)] = jnp.where(inside, sn, 0.0)

    def rotate(q):
        piece(q).wait()
        for u in range(run):
            c = q * run + u
            cs = row(cos_d, c)
            sn = row(sin_d, c)
            for part_i in range(2):
                up = wave[2 * part_i, :, at(c)]
                down = wave[2 * part_i + 1, :, at(c)]
                w[2 * part_i, :, at(c, 1)] = cs * up + sn * down
                w[2 * part_i + 1, :, at(c, 1)] = cs * down - sn * up

    site_terms(0)
    site_terms(chunks - 1)
    rotate(0)
    rotate(SHARES - 1)

    all_modes = float(modes * nm)
    root = 1.0 / math.sqrt(all_modes)
    weight = root * par[16]

    ends = []
    for edge, c, back in ((edge_r, chunks - 1, 4), (edge_l, 0, 0)):
        rows = zero
        for i in range(6):
            rows = jnp.where(sub == i, coef[i, :, c * LANES : (c + 1) * LANES], rows)
        packed = pltpu.roll(rows, 16 + back, 1)
        state = [w[i, :, (c + 1) * LANES : (c + 2) * LANES] for i in range(4)]
        for i in range(4):
            moved = pltpu.roll(state[i], 4 * i + back, 1) if i or back else state[i]
            packed = jnp.where((lane >= 4 * i) & (lane < 4 * i + 4), moved, packed)
        edge[...] = packed
        ends.append(state)
    left_factor = zero
    right_factor = zero
    for i in range(4):
        left_factor = jnp.where(lane == i, pltpu.roll(ends[0][i], 1 + i, 1), left_factor)
        other = ends[1][(i + 2) % 4]
        other = pltpu.roll(other, i, 1) if i else other
        right_factor = jnp.where(lane == i, other if i < 2 else -other, right_factor)
    bond_a[...] = 2.0 * (weight * left_factor)
    bond_b[...] = right_factor

    to_left = send(
        edge_l, halo_r, halo_send.at[0], halo_recv.at[0], {"sites": jnp.maximum(tile - 1, 0)}
    )
    to_right = send(
        edge_r, halo_l, halo_send.at[1], halo_recv.at[1], {"sites": jnp.minimum(tile + 1, ns - 1)}
    )
    to_keeper = send(bond_a, slots_a.at[me], a_send, a_recv, {"modes": keeper})
    to_left_keeper = send(
        bond_b,
        slots_b.at[me],
        b_send,
        b_recv,
        {"modes": left_keeper, "sites": jnp.maximum(tile - 1, 0)},
    )

    @pl.when(late)
    def _():
        to_right.start()

    @pl.when(has_left & jnp.logical_not(at_turn | before_turn))
    def _():
        to_left_keeper.start()

    @pl.when(has_left & jnp.logical_not(early))
    def _():
        to_left.start()

    @pl.when(jnp.logical_not(keeps))
    def _():
        to_keeper.start()

    def current(wc, wn, weight):
        after = [jnp.where(first, n, c) for c, n in zip(wc, wn)]
        after = [pltpu.roll(a, LANES - 1, 1) for a in after]
        return weight * (
            wc[0] * after[2] - wc[2] * after[0] + (wc[1] * after[3] - wc[3] * after[1])
        )

    def down_sum(x):
        return jnp.sum(x, axis=0, keepdims=True)

    odd = (sub & 1) == 1
    upper_pair = (sub & 2) == 2
    lower_half = sub < 4

    def fold(x, y, other, shift):
        return jnp.where(other, y, x) + pltpu.roll(jnp.where(other, x, y), 8 - shift, 0)

    def fold_four(x):
        return fold(fold(x[0], x[1], odd, 1), fold(x[2], x[3], odd, 1), upper_pair, 2)

    def fold_eight(x):
        return fold(fold_four(x[:4]), fold_four(x[4:]), jnp.logical_not(lower_half), 4)

    first_scale = jnp.where(lower_half, root, 2.0)
    second_scale = jnp.where(lower_half, 2.0, 1.0)

    def density(q):
        wc = [w[i, :, at(q * run, 1)] for i in range(4)]
        tiles = [[], [], [], [], []]
        for u in range(run):
            c = q * run + u
            wn = [w[i, :, at(c, 2)] for i in range(4)]
            ur, dr, ui, di = [wave[i, :, at(c)] for i in range(4)]
            wur, wdr, wui, wdi = [weight * x for x in (ur, dr, ui, di)]
            up = wur * ur + wui * ui
            dn = wdr * dr + wdi * di
            tiles[0].append(up + dn)
            tiles[1].append(wur * dr + wui * di)
            tiles[2].append(wur * di - wui * dr)
            tiles[3].append(up - dn)
            tiles[4].append(current(wc, wn, weight))
            wc = wn
        part[q, 0:8, :] = first_scale * fold_eight(tiles[0] + tiles[1])
        part[q, 8:16, :] = second_scale * fold_eight(tiles[2] + tiles[3])
        bonds = fold_four(tiles[4])
        part[q, 16:20, :] = (2.0 * (bonds + pltpu.roll(bonds, 4, 0)))[0:4, :]
        owner = owner_at(q)

        @pl.when(owner != me)
        def _():
            send(part.at[q], slots.at[q, me], rs_send.at[q], rs_recv.at[q], {"modes": owner}).start()

    def stream(q, carry):
        rotate(q)
        density(q - 1)
        return carry

    def finish(q, carry):
        density(q)
        return carry

    lax.fori_loop(1, SHARES - 1, stream, 0)
    lax.fori_loop(SHARES - 2, SHARES, finish, 0)

    @pl.when(before_turn)
    def _():
        pl.semaphore_wait(ready, 1)
        to_left_keeper.start()
        to_left.start()

    def stage_pass(src_ref, dst_ref, k):
        def body(block, carry):
            def load(c, shift):
                return [src_ref[i, :, at(c, shift)] for i in range(4)]

            c0 = block * unroll
            prev = load(c0, 0)
            here = load(c0, 1)
            for u in range(unroll):
                c = c0 + u
                after = load(c, 2)
                lefts = [pltpu.roll(jnp.where(last, p, h), 1, 1) for p, h in zip(prev, here)]
                rights = [
                    pltpu.roll(jnp.where(first, a, h), LANES - 1, 1) for a, h in zip(after, here)
                ]
                base = here if k == 3 else [w[i, :, at(c, 1)] for i in range(4)]
                out = apply_stage(
                    here,
                    lefts,
                    rights,
                    [coef[i, :, at(c)] for i in range(4)],
                    base,
                    STAGE_WEIGHT[k],
                    [par[4 * k + i] for i in range(4)],
                    [cmask[0, :, at(c)], cmask[1, :, at(c)]],
                )
                if k > 0:
                    for i in range(4):
                        dst_ref[i, :, at(c, 1)] = out[i]
                else:
                    cs = E4 * coef[4, :, at(c)]
                    sn = E4 * coef[5, :, at(c)]
                    for h in range(2):
                        next_out[2 * h, :, at(c)] = cs * out[2 * h] - sn * out[2 * h + 1]
                        next_out[2 * h + 1, :, at(c)] = sn * out[2 * h] + cs * out[2 * h + 1]
                prev, here = here, after
            return carry

        lax.fori_loop(0, chunks // unroll, body, 0)

    def terms(block, carry):
        for u in range(unroll):
            site_terms(block * unroll + u)
        return carry

    lax.fori_loop(0, chunks // unroll, terms, 0)
    stage_pass(w, ya, 3)
    stage_pass(ya, yb, 2)
    stage_pass(yb, ya, 1)

    @pl.when(has_right & jnp.logical_not(late))
    def _():
        to_left.wait_recv()
        to_right.start()

    def add_up(q, carry):
        owns = owner_at(q) == me

        @pl.when(owns)
        def _():
            slots[q, me] = part[q]
            pltpu.make_async_copy(
                slots.at[q, 0 : nm - 1], slots.at[q, 0 : nm - 1], rs_recv.at[q]
            ).wait()
            total = slots[q, 0]
            for d in range(1, nm):
                total = total + slots[q, d]
            sums[q] = total

            @pl.when(q == SHARES - 1)
            def _():
                pltpu.make_async_copy(
                    slots_a.at[0 : nm - 1], slots_a.at[0 : nm - 1], a_recv
                ).wait()

            @pl.when((q == SHARES - 1) & has_right)
            def _():
                pltpu.make_async_copy(slots_b, slots_b, b_recv).wait()
                bond = bond_a[...] * slots_b[me]
                for k in range(1, nm):
                    bond = bond + slots_a[me ^ k] * slots_b[me ^ k]
                bond = jnp.sum(down_sum(bond), axis=1, keepdims=True)
                end = 5 * run - 1
                sums[q, end : end + 1, :] = sums[q, end : end + 1, :] + jnp.where(
                    last[0:1], jnp.broadcast_to(bond, (1, LANES)), 0.0
                )

            for j in order:
                @pl.when(me != j)
                def _():
                    send(
                        sums.at[q],
                        sums.at[q],
                        ag_send.at[q],
                        ag_recv.at[q],
                        {"modes": jnp.int32(j)},
                    ).start()

        return carry

    lax.fori_loop(0, SHARES, add_up, 0)

    stage_pass(ya, None, 0)
    for i in range(3):
        for c in range(chunks):
            mag_d[i, c : c + 1, :] = mag[i : i + 1, c * LANES : (c + 1) * LANES]

    def redo_ends():
        @pl.when(has_left)
        def _():
            to_right.wait_recv()

        @pl.when(late)
        def _():
            to_left.wait_recv()

        base = []
        coefs = []
        masks = []
        alive = []
        for where in range(4):
            if where in (0, 3):
                halo = halo_l if where == 0 else halo_r
                there = has_left if where == 0 else has_right
                keep = jnp.full((8, LANES), there.astype(jnp.int32)) > 0
                alive.append(keep)
                back = 4 if where == 0 else 0
                packed = halo[...]
                state = [
                    pltpu.roll(packed, LANES - 4 * i - back, 1) if i or back else packed
                    for i in range(4)
                ]
                base.append([jnp.where(keep, x, 0.0) for x in state])
                rows = pltpu.roll(packed, LANES - 16 - back, 1)
                rows = [jnp.broadcast_to(rows[i : i + 1, :], (8, LANES)) for i in range(6)]
                coefs.append(rows[:4])
                start = tile * sites + (-LANES if where == 0 else sites)
                inside = in_region(start + lane)
                masks.append([jnp.where(inside, rows[4], 0.0), jnp.where(inside, rows[5], 0.0)])
            else:
                c = 0 if where == 1 else chunks - 1
                cut = slice(c * LANES, (c + 1) * LANES)
                alive.append(None)
                base.append([w[i, :, (c + 1) * LANES : (c + 2) * LANES] for i in range(4)])
                coefs.append([coef[i, :, cut] for i in range(4)])
                masks.append([cmask[0, :, cut], cmask[1, :, cut]])
        y = base
        for k in (3, 2, 1, 0):
            out = []
            for where in range(4):
                prev, here, after = y[(where + 3) % 4], y[where], y[(where + 1) % 4]
                lefts = [pltpu.roll(jnp.where(last, p, h), 1, 1) for p, h in zip(prev, here)]
                rights = [
                    pltpu.roll(jnp.where(first, a, h), LANES - 1, 1) for a, h in zip(after, here)
                ]
                new = apply_stage(
                    here,
                    lefts,
                    rights,
                    coefs[where],
                    base[where],
                    STAGE_WEIGHT[k],
                    [par[4 * k + i] for i in range(4)],
                    masks[where],
                )
                if alive[where] is not None:
                    new = [jnp.where(alive[where], x, 0.0) for x in new]
                out.append(new)
            y = out
        for where, c in ((1, 0), (2, chunks - 1)):
            cut = slice(c * LANES, (c + 1) * LANES)
            cs = E4 * coef[4, :, cut]
            sn = E4 * coef[5, :, cut]
            fresh = lane < 4 if where == 1 else lane >= LANES - 4
            for h in range(2):
                up = cs * y[where][2 * h] - sn * y[where][2 * h + 1]
                down = sn * y[where][2 * h] + cs * y[where][2 * h + 1]
                next_out[2 * h, :, cut] = jnp.where(fresh, up, next_out[2 * h, :, cut])
                next_out[2 * h + 1, :, cut] = jnp.where(fresh, down, next_out[2 * h + 1, :, cut])

    @pl.when(jnp.logical_not(early))
    def _():
        redo_ends()

    @pl.when(early & jnp.logical_not(before_turn))
    def _():
        pl.semaphore_wait(ready, 1)

    @pl.when(at_turn)
    def _():
        to_left_keeper.start()

    @pl.when(early & jnp.logical_not(before_turn))
    def _():
        to_left.start()

    for q in range(SHARES):
        @pl.when(owner_of(q) != me)
        def _():
            pltpu.make_async_copy(sums.at[q], sums.at[q], ag_recv.at[q]).wait()

        hx, hy, hz = [sums[q, i * run : (i + 1) * run, :] for i in (1, 2, 3)]
        m = [mag_d[i, q * run : (q + 1) * run, :] for i in range(3)]
        turn = time_step * half_d[q * run : (q + 1) * run, :]
        mag_n[0:run, :] = m[0] - turn * (m[1] * hz - m[2] * hy)
        mag_n[run : 2 * run, :] = m[1] - turn * (m[2] * hx - m[0] * hz)
        mag_n[2 * run : 3 * run, :] = m[2] - turn * (m[0] * hy - m[1] * hx)
        for u in range(run):
            cut = slice((q * run + u) * LANES, (q * run + u + 1) * LANES)
            dens_out[:, cut] = sums[q, pl.ds(u, 5, stride=run), :]
            magn_out[:, cut] = mag_n[pl.ds(u, 3, stride=run), :]

    @pl.when(early)
    def _():
        redo_ends()

    @pl.when(has_right)
    def _():
        to_right.wait_send()

    @pl.when(has_left)
    def _():
        to_left.wait_send()
        to_left_keeper.wait_send()

    @pl.when(jnp.logical_not(keeps))
    def _():
        to_keeper.wait_send()

    def settle(q, carry):
        @pl.when(owner_at(q) != me)
        def _():
            pltpu.make_async_copy(part.at[q], part.at[q], rs_send.at[q]).wait()

        @pl.when(owner_at(q) == me)
        def _():
            pltpu.make_async_copy(
                slots.at[q, 0 : nm - 1], slots.at[q, 0 : nm - 1], ag_send.at[q]
            ).wait()

        return carry

    lax.fori_loop(0, SHARES, settle, 0)


def hand_out(next_v, dens_v, magn_v, next_out, dens_out, magn_out, sem):
    copies = [
        pltpu.make_async_copy(src, dst, sem.at[i])
        for i, (src, dst) in enumerate(
            [(next_v, next_out), (dens_v, dens_out), (magn_v, magn_out)]
        )
    ]
    for copy in copies:
        copy.start()
    for copy in copies:
        copy.wait()


def solution(mesh):
    nm = mesh.shape["modes"]
    ns = mesh.shape["sites"]

    def local(
        wave_state,
        potential,
        spin_angle,
        magnet,
        magnetic_mask,
        mode_weight,
        source_amp,
        mode_group,
        energies,
        lead_site,
    ):
        sites = wave_state.shape[2]
        dense = (sites // LANES, LANES)
        modes = wave_state.shape[1]
        rows = 5 * dense[0] // SHARES
        f32 = jnp.float32
        vmem = pltpu.VMEM
        whole = pl.BlockSpec(memory_space=pl.ANY)
        kept = pl.BlockSpec(memory_space=pltpu.VMEM)
        out = pl.pallas_call(
            functools.partial(kernel, nm, ns, sites),
            out_shape=(
                jax.ShapeDtypeStruct(wave_state.shape, f32),
                jax.ShapeDtypeStruct((5, sites), f32),
                jax.ShapeDtypeStruct((3, sites), f32),
            ),
            in_specs=[whole] * 10,
            out_specs=(kept, kept, kept),
            scratch_shapes=[
                vmem(wave_state.shape, f32),
                vmem(dense, f32),
                vmem(dense, f32),
                vmem((3, sites), f32),
                vmem(dense, jnp.int32),
                vmem((1, modes), f32),
                vmem((4, modes), f32),
                vmem((1, modes), jnp.int32),
                vmem((1, energies.shape[0]), f32),
                vmem((1, modes), jnp.int32),
                vmem(dense, f32),
                vmem(dense, f32),
                vmem(dense, f32),
                vmem(dense, f32),
                vmem(dense, f32),
                vmem((3, *dense), f32),
                vmem((3 * rows // 5, LANES), f32),
                vmem((18, modes, LANES), f32),
                vmem((4, modes, sites + 2 * LANES), f32),
                vmem((4, modes, sites + 2 * LANES), f32),
                vmem((4, modes, sites + 2 * LANES), f32),
                vmem((6, modes, sites), f32),
                vmem((2, modes, sites), f32),
                vmem((modes, LANES), f32),
                vmem((modes, LANES), f32),
                vmem((modes, LANES), f32),
                vmem((modes, LANES), f32),
                vmem((modes, LANES), f32),
                vmem((modes, LANES), f32),
                vmem((nm, modes, LANES), f32),
                vmem((nm, modes, LANES), f32),
                vmem((SHARES, rows, LANES), f32),
                vmem((SHARES, nm, rows, LANES), f32),
                vmem((SHARES, rows, LANES), f32),
                pltpu.SemaphoreType.DMA((9,)),
                pltpu.SemaphoreType.DMA((SHARES,)),
                pltpu.SemaphoreType.DMA((2,)),
                pltpu.SemaphoreType.DMA((2,)),
                pltpu.SemaphoreType.DMA,
                pltpu.SemaphoreType.DMA,
                pltpu.SemaphoreType.DMA,
                pltpu.SemaphoreType.DMA,
                pltpu.SemaphoreType.DMA((SHARES,)),
                pltpu.SemaphoreType.DMA((SHARES,)),
                pltpu.SemaphoreType.DMA((SHARES,)),
                pltpu.SemaphoreType.DMA((SHARES,)),
                pltpu.SemaphoreType.REGULAR,
            ],
            compiler_params=pltpu.CompilerParams(
                collective_id=0,
                has_side_effects=True,
                vmem_limit_bytes=32 * 1024 * 1024,
            ),
        )(
            *[
                pltpu.with_memory_space_constraint(x, pltpu.HBM)
                for x in (
                    wave_state,
                    potential.reshape(dense),
                    spin_angle.reshape(dense),
                    magnet,
                    magnetic_mask.reshape(dense),
                    mode_weight.reshape(1, modes),
                    source_amp,
                    mode_group.reshape(1, modes),
                    energies.reshape(1, -1),
                    lead_site.reshape(1, modes),
                )
            ]
        )
        return pl.pallas_call(
            hand_out,
            out_shape=tuple(jax.ShapeDtypeStruct(x.shape, f32) for x in out),
            in_specs=[kept] * 3,
            out_specs=(whole,) * 3,
            scratch_shapes=[pltpu.SemaphoreType.DMA((3,))],
            compiler_params=pltpu.CompilerParams(vmem_limit_bytes=2 * 1024 * 1024),
        )(*out)

    return jax.shard_map(
        local,
        mesh=mesh,
        in_specs=(
            P(None, "modes", "sites"),
            P("sites"),
            P("sites"),
            P(None, "sites"),
            P("sites"),
            P("modes"),
            P(None, "modes"),
            P("modes"),
            P(),
            P("modes"),
        ),
        out_specs=(P(None, "modes", "sites"), P(None, "sites"), P(None, "sites")),
        check_vma=False,
    )
```

```python
import functools
import math

import jax
import jax.numpy as jnp
from jax import lax
from jax.experimental import pallas as pl
from jax.experimental.pallas import tpu as pltpu
from jax.sharding import PartitionSpec as P

time_step = 0.6
start_time = 10.0
exchange_coupling = 0.5
MESH = pl.DeviceIdType.MESH
LANES = 128
SHARES = 8
FIRST_TILE_OWNERS = {16: (1, 1, 1, 1, 2, 3, 4, 5), 4: (1, 1, 1, 1, 2, 2, 3, 3)}

E4 = time_step**4 / 24.0
STAGE_WEIGHT = [
    24.0 / time_step**4,
    24.0 / time_step**3,
    12.0 / time_step**2,
    4.0 / time_step,
]


def apply_stage(y, left, right, coef, base, weight, src, masks):
    ur, dr, ui, di = y
    a_up, a_dn, fx, fy = coef
    near = [l + r for l, r in zip(left, right)]
    h_ur = a_up * ur + fx * dr + fy * di - near[0]
    h_dr = a_dn * dr + fx * ur - fy * ui - near[1]
    h_ui = a_up * ui + fx * di - fy * dr - near[2]
    h_di = a_dn * di + fx * ui + fy * ur - near[3]
    cm, sm = masks
    src_ur = cm * src[0] + sm * src[1]
    src_dr = cm * src[1] - sm * src[0]
    src_ui = cm * src[2] + sm * src[3]
    src_di = cm * src[3] - sm * src[2]
    return [
        (weight * base[0] + src_ur) + h_ui,
        (weight * base[1] + src_dr) + h_di,
        (weight * base[2] + src_ui) - h_ur,
        (weight * base[3] + src_di) - h_dr,
    ]


def kernel(
    nm,
    ns,
    sites,
    wave_hbm,
    pot_hbm,
    ang_hbm,
    mag_hbm,
    mask_hbm,
    wt_hbm,
    amp_hbm,
    grp_hbm,
    en_hbm,
    lead_hbm,
    next_out,
    dens_out,
    magn_out,
    wave,
    pot,
    ang,
    mag,
    mask,
    wt,
    amp,
    grp,
    en,
    lead,
    cos_d,
    sin_d,
    cos2_d,
    sin2_d,
    half_d,
    mag_d,
    mag_n,
    par,
    w,
    ya,
    yb,
    coef,
    cmask,
    edge_l,
    edge_r,
    halo_l,
    halo_r,
    bond_a,
    bond_b,
    slots_a,
    slots_b,
    part,
    slots,
    sums,
    in_sem,
    wave_sem,
    halo_send,
    halo_recv,
    a_send,
    a_recv,
    b_send,
    b_recv,
    rs_send,
    rs_recv,
    ag_send,
    ag_recv,
    ready,
):
    chunks = sites // LANES
    run = chunks // SHARES
    unroll = 4
    me = lax.axis_index("modes")
    tile = lax.axis_index("sites")
    turn_tile = ns // 2
    has_left = tile > 0
    has_right = tile < ns - 1
    at_turn = tile == turn_tile
    before_turn = tile == turn_tile - 1
    early = at_turn | before_turn | ((tile == 1) & (me == 0))
    late = before_turn | (tile == turn_tile - 2) | ((tile == 0) & (me == 0))
    usual = [q * min(nm, SHARES) // SHARES for q in range(SHARES)]
    usual = [1, 3, 5, 7, 1, 3, 5, 7] if nm == 16 else usual
    special = FIRST_TILE_OWNERS.get(nm, usual)

    def owner_of(q):
        return jnp.where(tile == 0, jnp.int32(special[q]), jnp.int32(usual[q]))

    def owner_at(q):
        found = owner_of(0)
        for i in range(1, SHARES):
            found = jnp.where(q == i, owner_of(i), found)
        return found

    def among(devices):
        found = me == devices[0]
        for d in devices[1:]:
            found = found | (me == d)
        return found

    is_owner = jnp.where(tile == 0, among(sorted(set(special))).astype(jnp.int32), among(sorted(set(usual))).astype(jnp.int32))
    owner_count = jnp.where(tile == 0, len(set(special)), len(set(usual)))
    keeper = owner_of(SHARES - 1)
    keeps = me == keeper
    left_keeper = jnp.where(tile == 1, jnp.int32(special[-1]), jnp.int32(usual[-1]))
    order = [j for j in (1, 3, 0, 2, 5, 7, 4, 6, 13, 15, 12, 14, 9, 11, 8, 10) if j < nm]

    def signal(sem, where):
        pl.semaphore_signal(sem, inc=1, device_id=where, device_id_type=MESH)

    def send(src, dst, send_sem, recv_sem, where):
        return pltpu.make_async_remote_copy(
            src_ref=src,
            dst_ref=dst,
            send_sem=send_sem,
            recv_sem=recv_sem,
            device_id=where,
            device_id_type=MESH,
        )

    barrier = pltpu.get_barrier_semaphore()

    @pl.when(is_owner == 1)
    def _():
        for k in range(1, nm):
            signal(barrier, {"modes": me ^ k})

    @pl.when(has_right & jnp.logical_not(late))
    def _():
        signal(barrier, {"sites": tile + 1})

    @pl.when(early)
    def _():
        signal(barrier, {"sites": tile - 1})

    @pl.when(keeps & has_right & (tile != turn_tile - 2) & jnp.logical_not(before_turn))
    def _():
        for m in range(nm):
            signal(barrier, {"modes": jnp.int32(m), "sites": tile + 1})

    fetches = [
        pltpu.make_async_copy(src, dst, in_sem.at[i])
        for i, (src, dst) in enumerate(
            [
                (wt_hbm, wt),
                (amp_hbm, amp),
                (grp_hbm, grp),
                (en_hbm, en),
                (lead_hbm, lead),
                (ang_hbm, ang),
                (pot_hbm, pot),
                (mag_hbm, mag),
                (mask_hbm, mask),
            ]
        )
    ]

    def piece(q):
        cut = pl.ds(pl.multiple_of(q * (run * LANES), LANES), run * LANES)
        return pltpu.make_async_copy(
            wave_hbm.at[:, :, cut], wave.at[:, :, cut], wave_sem.at[q]
        )

    for fetch in fetches:
        fetch.start()
    for q in (0, SHARES - 1, *range(1, SHARES - 1)):
        piece(q).start()
    pl.semaphore_wait(
        barrier,
        owner_count
        - is_owner
        + (has_left & jnp.logical_not(early)).astype(jnp.int32)
        + (has_left & jnp.logical_not(at_turn | before_turn)).astype(jnp.int32)
        + late.astype(jnp.int32),
    )

    @pl.when(late)
    def _():
        signal(ready, {"sites": tile + 1})

    for fetch in fetches[:5]:
        fetch.wait()

    modes = wt.shape[1]
    diag = lax.broadcasted_iota(jnp.int32, (modes, modes), 0) == lax.broadcasted_iota(
        jnp.int32, (modes, modes), 1
    )

    def column(row):
        spread = jnp.where(diag, jnp.broadcast_to(row, (modes, modes)), 0.0)
        return jnp.broadcast_to(jnp.sum(spread, axis=1, keepdims=True), (modes, LANES))

    par[16] = column(wt[...])
    par[17] = column(lead[...].astype(jnp.float32))

    for fetch in fetches[5:9]:
        fetch.wait()
    angle = ang[...]
    cosine = jnp.cos(angle)
    sine = jnp.sin(angle)
    cos_d[...] = cosine
    sin_d[...] = sine
    cos2_d[...] = 1.0 - 2.0 * sine * sine
    sin2_d[...] = 2.0 * sine * cosine
    half_d[...] = exchange_coupling * mask[...].astype(jnp.float32)

    zero = jnp.zeros((8, LANES), jnp.float32)
    for buf in (w, ya, yb):
        for c in range(4):
            buf[c, :, 0:LANES] = zero
            buf[c, :, LANES + sites : 2 * LANES + sites] = zero
    lane = lax.broadcasted_iota(jnp.int32, (8, LANES), 1)
    sub = lax.broadcasted_iota(jnp.int32, (8, LANES), 0)
    first = lane == 0
    last = lane == LANES - 1
    span = float(sites * ns // 8)

    def in_region(position):
        away = position.astype(jnp.float32) - par[17]
        return (away >= 0.0) & (away < span)

    def row(ref, i):
        return jnp.broadcast_to(ref[pl.ds(i, 1), :], (8, LANES))

    def at(c, shift=0):
        return pl.ds(pl.multiple_of(c * LANES, LANES) + shift * LANES, LANES)

    def site_terms(c):
        cs = row(cos_d, c)
        sn = row(sin_d, c)
        c2 = row(cos2_d, c)
        s2 = row(sin2_d, c)
        half = row(half_d, c)
        field = [half * jnp.broadcast_to(mag[i : i + 1, at(c)], (8, LANES)) for i in range(3)]
        v = row(pot, c)
        fz = c2 * field[2] + s2 * field[0]
        coef[0, :, at(c)] = v + fz
        coef[1, :, at(c)] = v - fz
        coef[2, :, at(c)] = c2 * field[0] - s2 * field[2]
        coef[3, :, at(c)] = field[1]
        coef[4, :, at(c)] = cs
        coef[5, :, at(c)] = sn
        inside = in_region(tile * sites + c * LANES + lane)
        cmask[0, :, at(c)] = jnp.where(inside, cs, 0.0)
        cmask[1, :, at(c)] = jnp.where(inside, sn, 0.0)

    def rotate(q):
        piece(q).wait()
        for u in range(run):
            c = q * run + u
            cs = row(cos_d, c)
            sn = row(sin_d, c)
            for part_i in range(2):
                up = wave[2 * part_i, :, at(c)]
                down = wave[2 * part_i + 1, :, at(c)]
                w[2 * part_i, :, at(c, 1)] = cs * up + sn * down
                w[2 * part_i + 1, :, at(c, 1)] = cs * down - sn * up

    site_terms(0)
    site_terms(chunks - 1)
    rotate(0)
    rotate(SHARES - 1)

    all_modes = float(modes * nm)
    root = 1.0 / math.sqrt(all_modes)
    weight = root * par[16]

    ends = []
    for edge, c, back in ((edge_r, chunks - 1, 4), (edge_l, 0, 0)):
        rows = zero
        for i in range(6):
            rows = jnp.where(sub == i, coef[i, :, c * LANES : (c + 1) * LANES], rows)
        packed = pltpu.roll(rows, 16 + back, 1)
        state = [w[i, :, (c + 1) * LANES : (c + 2) * LANES] for i in range(4)]
        for i in range(4):
            moved = pltpu.roll(state[i], 4 * i + back, 1) if i or back else state[i]
            packed = jnp.where((lane >= 4 * i) & (lane < 4 * i + 4), moved, packed)
        edge[...] = packed
        ends.append(state)
    left_factor = zero
    right_factor = zero
    for i in range(4):
        left_factor = jnp.where(lane == i, pltpu.roll(ends[0][i], 1 + i, 1), left_factor)
        other = ends[1][(i + 2) % 4]
        other = pltpu.roll(other, i, 1) if i else other
        right_factor = jnp.where(lane == i, other if i < 2 else -other, right_factor)
    bond_a[...] = 2.0 * (weight * left_factor)
    bond_b[...] = right_factor

    to_left = send(
        edge_l, halo_r, halo_send.at[0], halo_recv.at[0], {"sites": jnp.maximum(tile - 1, 0)}
    )
    to_right = send(
        edge_r, halo_l, halo_send.at[1], halo_recv.at[1], {"sites": jnp.minimum(tile + 1, ns - 1)}
    )
    to_keeper = send(bond_a, slots_a.at[me], a_send, a_recv, {"modes": keeper})
    to_left_keeper = send(
        bond_b,
        slots_b.at[me],
        b_send,
        b_recv,
        {"modes": left_keeper, "sites": jnp.maximum(tile - 1, 0)},
    )

    @pl.when(late)
    def _():
        to_right.start()

    @pl.when(has_left & jnp.logical_not(at_turn | before_turn))
    def _():
        to_left_keeper.start()

    @pl.when(has_left & jnp.logical_not(early))
    def _():
        to_left.start()

    @pl.when(jnp.logical_not(keeps))
    def _():
        to_keeper.start()

    def current(wc, wn, weight):
        after = [jnp.where(first, n, c) for c, n in zip(wc, wn)]
        after = [pltpu.roll(a, LANES - 1, 1) for a in after]
        return weight * (
            wc[0] * after[2] - wc[2] * after[0] + (wc[1] * after[3] - wc[3] * after[1])
        )

    def down_sum(x):
        return jnp.sum(x, axis=0, keepdims=True)

    odd = (sub & 1) == 1
    upper_pair = (sub & 2) == 2
    lower_half = sub < 4

    def fold(x, y, other, shift):
        return jnp.where(other, y, x) + pltpu.roll(jnp.where(other, x, y), 8 - shift, 0)

    def fold_four(x):
        return fold(fold(x[0], x[1], odd, 1), fold(x[2], x[3], odd, 1), upper_pair, 2)

    def fold_eight(x):
        return fold(fold_four(x[:4]), fold_four(x[4:]), jnp.logical_not(lower_half), 4)

    first_scale = jnp.where(lower_half, root, 2.0)
    second_scale = jnp.where(lower_half, 2.0, 1.0)

    def density(q):
        wc = [w[i, :, at(q * run, 1)] for i in range(4)]
        tiles = [[], [], [], [], []]
        for u in range(run):
            c = q * run + u
            wn = [w[i, :, at(c, 2)] for i in range(4)]
            ur, dr, ui, di = [wave[i, :, at(c)] for i in range(4)]
            wur, wdr, wui, wdi = [weight * x for x in (ur, dr, ui, di)]
            up = wur * ur + wui * ui
            dn = wdr * dr + wdi * di
            tiles[0].append(up + dn)
            tiles[1].append(wur * dr + wui * di)
            tiles[2].append(wur * di - wui * dr)
            tiles[3].append(up - dn)
            tiles[4].append(current(wc, wn, weight))
            wc = wn
        part[q, 0:8, :] = first_scale * fold_eight(tiles[0] + tiles[1])
        part[q, 8:16, :] = second_scale * fold_eight(tiles[2] + tiles[3])
        bonds = fold_four(tiles[4])
        part[q, 16:20, :] = (2.0 * (bonds + pltpu.roll(bonds, 4, 0)))[0:4, :]
        owner = owner_at(q)

        @pl.when(owner != me)
        def _():
            send(part.at[q], slots.at[q, me], rs_send.at[q], rs_recv.at[q], {"modes": owner}).start()

    def stream(q, carry):
        rotate(q)
        density(q - 1)
        return carry

    def finish(q, carry):
        density(q)
        return carry

    lax.fori_loop(1, SHARES - 1, stream, 0)
    lax.fori_loop(SHARES - 2, SHARES, finish, 0)

    @pl.when(before_turn)
    def _():
        pl.semaphore_wait(ready, 1)
        to_left_keeper.start()
        to_left.start()

    def stage_pass(src_ref, dst_ref, k):
        def body(block, carry):
            def load(c, shift):
                return [src_ref[i, :, at(c, shift)] for i in range(4)]

            c0 = block * unroll
            prev = load(c0, 0)
            here = load(c0, 1)
            for u in range(unroll):
                c = c0 + u
                after = load(c, 2)
                lefts = [pltpu.roll(jnp.where(last, p, h), 1, 1) for p, h in zip(prev, here)]
                rights = [
                    pltpu.roll(jnp.where(first, a, h), LANES - 1, 1) for a, h in zip(after, here)
                ]
                base = here if k == 3 else [w[i, :, at(c, 1)] for i in range(4)]
                out = apply_stage(
                    here,
                    lefts,
                    rights,
                    [coef[i, :, at(c)] for i in range(4)],
                    base,
                    STAGE_WEIGHT[k],
                    [par[4 * k + i] for i in range(4)],
                    [cmask[0, :, at(c)], cmask[1, :, at(c)]],
                )
                if k > 0:
                    for i in range(4):
                        dst_ref[i, :, at(c, 1)] = out[i]
                else:
                    cs = E4 * coef[4, :, at(c)]
                    sn = E4 * coef[5, :, at(c)]
                    for h in range(2):
                        next_out[2 * h, :, at(c)] = cs * out[2 * h] - sn * out[2 * h + 1]
                        next_out[2 * h + 1, :, at(c)] = sn * out[2 * h] + cs * out[2 * h + 1]
                prev, here = here, after
            return carry

        lax.fori_loop(0, chunks // unroll, body, 0)

    group = grp[...]
    energy_row = en[...]
    energy = jnp.zeros(group.shape, jnp.float32)
    for g in range(energy_row.shape[1]):
        energy = energy + jnp.where(group == g, energy_row[:, g : g + 1], 0.0)
    amp_re = amp[0:2, :]
    amp_im = amp[2:4, :]
    rate = []
    for offset in (0.0, 0.5 * time_step, time_step):
        phase = energy * (start_time + offset)
        cosine = jnp.cos(phase)
        sine = jnp.sin(phase)
        rate.append(
            (
                amp_im * cosine - amp_re * sine,
                -(amp_re * cosine + amp_im * sine),
            )
        )
    mixes = [
        [time_step / 6.0, 4.0 * time_step / 6.0, time_step / 6.0],
        [time_step / 6.0, 2.0 * time_step / 6.0, 0.0],
        [time_step / 6.0, time_step / 6.0, 0.0],
        [time_step / 4.0, 0.0, 0.0],
    ]
    for k in range(4):
        for half in range(2):
            mixed = sum(
                (STAGE_WEIGHT[k] * mixes[k][t]) * rate[t][half]
                for t in range(3)
                if mixes[k][t] != 0.0
            )
            for spin in range(2):
                par[4 * k + 2 * half + spin] = column(mixed[spin : spin + 1, :])
    def terms(block, carry):
        for u in range(unroll):
            site_terms(block * unroll + u)
        return carry

    lax.fori_loop(0, chunks // unroll, terms, 0)
    stage_pass(w, ya, 3)
    stage_pass(ya, yb, 2)
    stage_pass(yb, ya, 1)

    @pl.when(has_right & jnp.logical_not(late))
    def _():
        to_left.wait_recv()
        to_right.start()

    def add_up(q, carry):
        owns = owner_at(q) == me

        @pl.when(owns)
        def _():
            slots[q, me] = part[q]
            pltpu.make_async_copy(
                slots.at[q, 0 : nm - 1], slots.at[q, 0 : nm - 1], rs_recv.at[q]
            ).wait()
            total = slots[q, 0]
            for d in range(1, nm):
                total = total + slots[q, d]
            sums[q] = total

            @pl.when(q == SHARES - 1)
            def _():
                pltpu.make_async_copy(
                    slots_a.at[0 : nm - 1], slots_a.at[0 : nm - 1], a_recv
                ).wait()

            @pl.when((q == SHARES - 1) & has_right)
            def _():
                pltpu.make_async_copy(slots_b, slots_b, b_recv).wait()
                bond = bond_a[...] * slots_b[me]
                for k in range(1, nm):
                    bond = bond + slots_a[me ^ k] * slots_b[me ^ k]
                bond = jnp.sum(down_sum(bond), axis=1, keepdims=True)
                end = 5 * run - 1
                sums[q, end : end + 1, :] = sums[q, end : end + 1, :] + jnp.where(
                    last[0:1], jnp.broadcast_to(bond, (1, LANES)), 0.0
                )

            for j in order:
                @pl.when(me != j)
                def _():
                    send(
                        sums.at[q],
                        sums.at[q],
                        ag_send.at[q],
                        ag_recv.at[q],
                        {"modes": jnp.int32(j)},
                    ).start()

        return carry

    lax.fori_loop(0, SHARES, add_up, 0)

    stage_pass(ya, None, 0)
    for i in range(3):
        for c in range(chunks):
            mag_d[i, c : c + 1, :] = mag[i : i + 1, c * LANES : (c + 1) * LANES]

    def redo_ends():
        @pl.when(has_left)
        def _():
            to_right.wait_recv()

        @pl.when(late)
        def _():
            to_left.wait_recv()

        base = []
        coefs = []
        masks = []
        alive = []
        for where in range(4):
            if where in (0, 3):
                halo = halo_l if where == 0 else halo_r
                there = has_left if where == 0 else has_right
                keep = jnp.full((8, LANES), there.astype(jnp.int32)) > 0
                alive.append(keep)
                back = 4 if where == 0 else 0
                packed = halo[...]
                state = [
                    pltpu.roll(packed, LANES - 4 * i - back, 1) if i or back else packed
                    for i in range(4)
                ]
                base.append([jnp.where(keep, x, 0.0) for x in state])
                rows = pltpu.roll(packed, LANES - 16 - back, 1)
                rows = [jnp.broadcast_to(rows[i : i + 1, :], (8, LANES)) for i in range(6)]
                coefs.append(rows[:4])
                start = tile * sites + (-LANES if where == 0 else sites)
                inside = in_region(start + lane)
                masks.append([jnp.where(inside, rows[4], 0.0), jnp.where(inside, rows[5], 0.0)])
            else:
                c = 0 if where == 1 else chunks - 1
                cut = slice(c * LANES, (c + 1) * LANES)
                alive.append(None)
                base.append([w[i, :, (c + 1) * LANES : (c + 2) * LANES] for i in range(4)])
                coefs.append([coef[i, :, cut] for i in range(4)])
                masks.append([cmask[0, :, cut], cmask[1, :, cut]])
        y = base
        for k in (3, 2, 1, 0):
            out = []
            for where in range(4):
                prev, here, after = y[(where + 3) % 4], y[where], y[(where + 1) % 4]
                lefts = [pltpu.roll(jnp.where(last, p, h), 1, 1) for p, h in zip(prev, here)]
                rights = [
                    pltpu.roll(jnp.where(first, a, h), LANES - 1, 1) for a, h in zip(after, here)
                ]
                new = apply_stage(
                    here,
                    lefts,
                    rights,
                    coefs[where],
                    base[where],
                    STAGE_WEIGHT[k],
                    [par[4 * k + i] for i in range(4)],
                    masks[where],
                )
                if alive[where] is not None:
                    new = [jnp.where(alive[where], x, 0.0) for x in new]
                out.append(new)
            y = out
        for where, c in ((1, 0), (2, chunks - 1)):
            cut = slice(c * LANES, (c + 1) * LANES)
            cs = E4 * coef[4, :, cut]
            sn = E4 * coef[5, :, cut]
            fresh = lane < 4 if where == 1 else lane >= LANES - 4
            for h in range(2):
                up = cs * y[where][2 * h] - sn * y[where][2 * h + 1]
                down = sn * y[where][2 * h] + cs * y[where][2 * h + 1]
                next_out[2 * h, :, cut] = jnp.where(fresh, up, next_out[2 * h, :, cut])
                next_out[2 * h + 1, :, cut] = jnp.where(fresh, down, next_out[2 * h + 1, :, cut])

    @pl.when(jnp.logical_not(early))
    def _():
        redo_ends()

    @pl.when(early & jnp.logical_not(before_turn))
    def _():
        pl.semaphore_wait(ready, 1)

    @pl.when(at_turn)
    def _():
        to_left_keeper.start()

    @pl.when(early & jnp.logical_not(before_turn))
    def _():
        to_left.start()

    for q in range(SHARES):
        @pl.when(owner_of(q) != me)
        def _():
            pltpu.make_async_copy(sums.at[q], sums.at[q], ag_recv.at[q]).wait()

        hx, hy, hz = [sums[q, i * run : (i + 1) * run, :] for i in (1, 2, 3)]
        m = [mag_d[i, q * run : (q + 1) * run, :] for i in range(3)]
        turn = time_step * half_d[q * run : (q + 1) * run, :]
        mag_n[0:run, :] = m[0] - turn * (m[1] * hz - m[2] * hy)
        mag_n[run : 2 * run, :] = m[1] - turn * (m[2] * hx - m[0] * hz)
        mag_n[2 * run : 3 * run, :] = m[2] - turn * (m[0] * hy - m[1] * hx)
        for u in range(run):
            cut = slice((q * run + u) * LANES, (q * run + u + 1) * LANES)
            dens_out[:, cut] = sums[q, pl.ds(u, 5, stride=run), :]
            magn_out[:, cut] = mag_n[pl.ds(u, 3, stride=run), :]

    @pl.when(early)
    def _():
        redo_ends()

    @pl.when(has_right)
    def _():
        to_right.wait_send()

    @pl.when(has_left)
    def _():
        to_left.wait_send()
        to_left_keeper.wait_send()

    @pl.when(jnp.logical_not(keeps))
    def _():
        to_keeper.wait_send()

    def settle(q, carry):
        @pl.when(owner_at(q) != me)
        def _():
            pltpu.make_async_copy(part.at[q], part.at[q], rs_send.at[q]).wait()

        @pl.when(owner_at(q) == me)
        def _():
            pltpu.make_async_copy(
                slots.at[q, 0 : nm - 1], slots.at[q, 0 : nm - 1], ag_send.at[q]
            ).wait()

        return carry

    lax.fori_loop(0, SHARES, settle, 0)


def hand_out(next_v, dens_v, magn_v, next_out, dens_out, magn_out, sem):
    copies = [
        pltpu.make_async_copy(src, dst, sem.at[i])
        for i, (src, dst) in enumerate(
            [(next_v, next_out), (dens_v, dens_out), (magn_v, magn_out)]
        )
    ]
    for copy in copies:
        copy.start()
    for copy in copies:
        copy.wait()


def solution(mesh):
    nm = mesh.shape["modes"]
    ns = mesh.shape["sites"]

    def local(
        wave_state,
        potential,
        spin_angle,
        magnet,
        magnetic_mask,
        mode_weight,
        source_amp,
        mode_group,
        energies,
        lead_site,
    ):
        sites = wave_state.shape[2]
        dense = (sites // LANES, LANES)
        modes = wave_state.shape[1]
        rows = 5 * dense[0] // SHARES
        f32 = jnp.float32
        vmem = pltpu.VMEM
        whole = pl.BlockSpec(memory_space=pl.ANY)
        kept = pl.BlockSpec(memory_space=pltpu.VMEM)
        out = pl.pallas_call(
            functools.partial(kernel, nm, ns, sites),
            out_shape=(
                jax.ShapeDtypeStruct(wave_state.shape, f32),
                jax.ShapeDtypeStruct((5, sites), f32),
                jax.ShapeDtypeStruct((3, sites), f32),
            ),
            in_specs=[whole] * 10,
            out_specs=(kept, kept, kept),
            scratch_shapes=[
                vmem(wave_state.shape, f32),
                vmem(dense, f32),
                vmem(dense, f32),
                vmem((3, sites), f32),
                vmem(dense, jnp.int32),
                vmem((1, modes), f32),
                vmem((4, modes), f32),
                vmem((1, modes), jnp.int32),
                vmem((1, energies.shape[0]), f32),
                vmem((1, modes), jnp.int32),
                vmem(dense, f32),
                vmem(dense, f32),
                vmem(dense, f32),
                vmem(dense, f32),
                vmem(dense, f32),
                vmem((3, *dense), f32),
                vmem((3 * rows // 5, LANES), f32),
                vmem((18, modes, LANES), f32),
                vmem((4, modes, sites + 2 * LANES), f32),
                vmem((4, modes, sites + 2 * LANES), f32),
                vmem((4, modes, sites + 2 * LANES), f32),
                vmem((6, modes, sites), f32),
                vmem((2, modes, sites), f32),
                vmem((modes, LANES), f32),
                vmem((modes, LANES), f32),
                vmem((modes, LANES), f32),
                vmem((modes, LANES), f32),
                vmem((modes, LANES), f32),
                vmem((modes, LANES), f32),
                vmem((nm, modes, LANES), f32),
                vmem((nm, modes, LANES), f32),
                vmem((SHARES, rows, LANES), f32),
                vmem((SHARES, nm, rows, LANES), f32),
                vmem((SHARES, rows, LANES), f32),
                pltpu.SemaphoreType.DMA((9,)),
                pltpu.SemaphoreType.DMA((SHARES,)),
                pltpu.SemaphoreType.DMA((2,)),
                pltpu.SemaphoreType.DMA((2,)),
                pltpu.SemaphoreType.DMA,
                pltpu.SemaphoreType.DMA,
                pltpu.SemaphoreType.DMA,
                pltpu.SemaphoreType.DMA,
                pltpu.SemaphoreType.DMA((SHARES,)),
                pltpu.SemaphoreType.DMA((SHARES,)),
                pltpu.SemaphoreType.DMA((SHARES,)),
                pltpu.SemaphoreType.DMA((SHARES,)),
                pltpu.SemaphoreType.REGULAR,
            ],
            compiler_params=pltpu.CompilerParams(
                collective_id=0,
                has_side_effects=True,
                vmem_limit_bytes=32 * 1024 * 1024,
            ),
        )(
            *[
                pltpu.with_memory_space_constraint(x, pltpu.HBM)
                for x in (
                    wave_state,
                    potential.reshape(dense),
                    spin_angle.reshape(dense),
                    magnet,
                    magnetic_mask.reshape(dense),
                    mode_weight.reshape(1, modes),
                    source_amp,
                    mode_group.reshape(1, modes),
                    energies.reshape(1, -1),
                    lead_site.reshape(1, modes),
                )
            ]
        )
        return pl.pallas_call(
            hand_out,
            out_shape=tuple(jax.ShapeDtypeStruct(x.shape, f32) for x in out),
            in_specs=[kept] * 3,
            out_specs=(whole,) * 3,
            scratch_shapes=[pltpu.SemaphoreType.DMA((3,))],
            compiler_params=pltpu.CompilerParams(vmem_limit_bytes=2 * 1024 * 1024),
        )(*out)

    return jax.shard_map(
        local,
        mesh=mesh,
        in_specs=(
            P(None, "modes", "sites"),
            P("sites"),
            P("sites"),
            P(None, "sites"),
            P("sites"),
            P("modes"),
            P(None, "modes"),
            P("modes"),
            P(),
            P("modes"),
        ),
        out_specs=(P(None, "modes", "sites"), P(None, "sites"), P(None, "sites")),
        check_vma=False,
    )
```
